32 devices in a mesh: groups: 2 (over y), outer: 4 (over z), local: 4 (over x, core).
Axes of the slice: x: 2, y: 2, z: 4, core: 2. Of those that a mesh axis runs over, the one named last changes fastest.
Arguments:
- tokens: bfloat16 [2048, 3584], P(('groups', 'outer', 'local')), parts along dimension 0, may hold values from -6 to 6
- routes: int32 [2048, 8], P(('groups', 'outer', 'local')), parts along dimension 0, may hold values from 0 to 31, as said below
- combine_fixed: int32 [2048, 8], P(('groups', 'outer', 'local')), parts along dimension 0, may hold values from 1 to 65535
- gate_weight: bfloat16 [4, 3584, 1024], P('outer', None, 'local'), may hold values from -0.09375 to 0.09375
- up_weight: bfloat16 [4, 3584, 1024], P('outer', None, 'local'), may hold values from -0.09375 to 0.09375
- down_weight: bfloat16 [4, 1024, 3584], P('outer', None, 'local'), may hold values from -0.1875 to 0.1875
Outputs:
- combined: float32 [2048, 3584], P(('groups', 'outer', 'local')), parts along dimension 0
The draws below stay inside these ranges and needn't reach their ends.
There are 2 independent parts, one for each index of `groups`. The reference program is written for one: setup_inputs(seed, part) draws one part's arguments, and reference() takes and returns one part's arrays. A program takes and returns all parts, laid end to end along the dimension named above; an argument that names none is the same for every part. Nothing has to cross between parts.
Inputs may be any that keep to these rules, and one draw needn't show every extreme that they name: `routes`: each row names 8 different experts, lying in at most 4 pods (expert e lies in pod e // 8). The tokens of one device name the round's expert of one pod (an e with e % 8 == 0) at most 24 times, and on every device some pod reaches 24. `combine_fixed`: A route's combine weight is this value times 2**-16.
All inputs are finite; a program needn't handle non-finite values.
Results may differ from the reference program's by a relative error of at most 0.004.
Values may be sent and summed in bfloat16 or wider, within the bound.
No kernel may reach another device: no remote copies, remote signals or barrier semaphores. Data moves between devices by JAX's collectives and lax.ppermute only.
A program may use at most 64 MiB of HBM per device.

```python
import jax
import jax.numpy as jnp
from jax import lax

D = 3584
FF = 1024
TOP = 8
EXP_POD = 8
TOK_DEV = 64
EXPERTS = 32
TOKENS = 1024
N_OUTER = 4
N_LOCAL = 4


def draw_routes(key, part):
    key = jax.random.fold_in(key, 7)
    pod_count = EXPERTS // EXP_POD
    blocks = TOKENS // TOK_DEV
    key_perm, key_flag, key_first, key_step, key_order, key_force = jax.random.split(key, 6)
    orders = jax.vmap(lambda sub_key: jax.random.permutation(sub_key, TOK_DEV))(jax.random.split(key_perm, blocks))
    base_pod = (orders % pod_count).astype(jnp.int32)
    allowed = orders // pod_count % 2 == 0
    forced_pod = jax.random.randint(key_force, (1, 1), 0, pod_count)
    second_hit = jax.random.randint(key_flag, (blocks, TOK_DEV), 0, 2)
    second_hit = jnp.where(base_pod == forced_pod, 1, second_hit)
    second_hit = jnp.where(allowed, second_hit, 0)
    first_slot = jax.random.randint(key_first, (blocks, TOK_DEV, 4), 1, EXP_POD)
    stride = jax.random.randint(key_step, (blocks, TOK_DEV, 4), 1, EXP_POD - 1)
    other_slot = 1 + (first_slot - 1 + stride) % (EXP_POD - 1)
    lead_slot = jnp.stack([jnp.zeros_like(second_hit), jnp.where(second_hit == 1, 0, other_slot[:, :, 1]), other_slot[:, :, 2], other_slot[:, :, 3]], axis=2)
    offsets = jnp.arange(4, dtype=jnp.int32)
    pod_ids = (base_pod[:, :, None] + offsets[None, None, :]) % pod_count
    chosen = jnp.concatenate([pod_ids * EXP_POD + lead_slot, pod_ids * EXP_POD + first_slot], axis=2).reshape(TOKENS, TOP)
    column_order = jax.vmap(lambda sub_key: jax.random.permutation(sub_key, TOP))(jax.random.split(key_order, TOKENS))
    return jnp.take_along_axis(chosen, column_order, axis=1).astype(jnp.int32)


def with_ends(drawn, stream_key, low, largest):
    dims = drawn.shape
    index_at = [jax.random.randint(jax.random.fold_in(stream_key, axis), (), 0, dims[axis]) for axis in range(len(dims))]
    drawn = drawn.at[tuple(index_at)].set(low)
    longest = dims.index(max(dims))
    index_at[longest] = (index_at[longest] + 1) % dims[longest]
    return drawn.at[tuple(index_at)].set(largest)


def steps_of(stream_key, dims, shards, least, top_value):
    level, own = 1.0, jax.random.fold_in(stream_key, 6)
    for axis_at, parts in shards:
        steps = jnp.exp(jax.random.uniform(jax.random.fold_in(own, axis_at), (parts,), jnp.float32, least / len(shards), top_value / len(shards)))
        level = level * jnp.repeat(steps, dims[axis_at] // parts).reshape([-1 if axis == axis_at else 1 for axis in range(len(dims))])
    return level


def gaussian(own_key, shape, deviation, most, cuts=(), kind=jnp.bfloat16):
    values = deviation * jax.random.normal(own_key, shape, jnp.float32)
    if cuts:
        values = values * steps_of(own_key, shape, cuts, -0.22, 0.18)
    return jnp.clip(values, -most, most).astype(kind)


def setup_inputs(seed: int = 0, part: int = 0) -> dict:
    arg_keys = jax.random.split(jax.random.key(seed), 7)
    part_splits = jax.random.split(jax.random.fold_in(arg_keys[6], part), 7)
    tokens = gaussian(part_splits[0], (TOKENS, D), 1.0, 6.0, ((0, 16),))
    routes = draw_routes(jax.random.fold_in(jax.random.fold_in(arg_keys[6], part), 71), part)
    combine_fixed = with_ends(jax.random.randint(part_splits[2], (TOKENS, TOP), 1, 65536), jax.random.fold_in(part_splits[2], 1), 1, 65535).astype(jnp.int32)
    gate_weight = gaussian(arg_keys[3], (N_OUTER, D, FF), D ** -0.5, 0.09375, ((0, 4), (2, 4)))
    up_weight = gaussian(arg_keys[4], (N_OUTER, D, FF), D ** -0.5, 0.09375, ((0, 4), (2, 4)))
    down_weight = gaussian(arg_keys[5], (N_OUTER, FF, D), FF ** -0.5, 0.1875, ((0, 4), (2, 4)))
    return {"tokens": tokens, "routes": routes, "combine_fixed": combine_fixed, "gate_weight": gate_weight, "up_weight": up_weight, "down_weight": down_weight}


def reference(tokens, routes, combine_fixed, gate_weight, up_weight, down_weight):
    route_share = combine_fixed.astype(jnp.float32) * (1.0 / 65536.0)
    row_limit = N_OUTER * N_LOCAL * (3 * TOK_DEV // (2 * N_OUTER))

    def one_pod(combined, pod_index):
        target = pod_index * EXP_POD
        weight_col = jnp.sum(jnp.where(routes == target, route_share, 0.0), axis=1)
        is_live = jnp.any(routes == target, axis=1)
        picked = jnp.nonzero(is_live, size=row_limit, fill_value=0)[0].astype(jnp.int32)
        valid = jnp.arange(row_limit, dtype=jnp.int32) < jnp.sum(is_live.astype(jnp.int32))
        row_block = tokens[picked]
        gate_proj = jnp.dot(row_block, gate_weight[pod_index], preferred_element_type=jnp.float32)
        up_proj = jnp.dot(row_block, up_weight[pod_index], preferred_element_type=jnp.float32)
        hidden = (jax.nn.silu(gate_proj) * up_proj).astype(jnp.bfloat16)
        expert_out = jnp.dot(hidden, down_weight[pod_index], preferred_element_type=jnp.float32).astype(jnp.bfloat16)
        expert_out = lax.optimization_barrier(expert_out).astype(jnp.float32)
        scaled = jnp.where(valid, weight_col[picked], 0.0)[:, None] * expert_out
        return combined.at[picked].add(scaled), None

    start_value = jnp.zeros((TOKENS, D), jnp.float32)
    combined, unused = lax.scan(one_pod, start_value, jnp.arange(N_OUTER, dtype=jnp.int32))
    return combined
```

```python
import jax
import jax.numpy as jnp
from jax import lax
from jax.sharding import PartitionSpec as P

EXP_POD = 8


def per_device(tokens, routes, combine_fixed, gate_weight, up_weight, down_weight):
    tok_rows, width = tokens.shape
    n_out = lax.axis_size("outer")
    n_loc = lax.axis_size("local")
    capacity = 3 * tok_rows // (2 * n_out)
    part_out = down_weight.shape[2]
    part_hid = gate_weight.shape[2]
    z = lax.axis_index("outer")
    l = lax.axis_index("local")
    gate_local = gate_weight[0]
    up_local = up_weight[0]
    down_local = jnp.concatenate(
        [lax.dynamic_slice_in_dim(down_weight[0], (l ^ m) * part_hid, part_hid, 0) for m in range(n_loc)], axis=0
    )

    targets = (z ^ jnp.arange(n_out, dtype=jnp.int32)) * EXP_POD
    hit_mask = routes[:, :, None] == targets[None, None, :]
    fixed = jnp.sum(jnp.where(hit_mask, combine_fixed[:, :, None], 0), axis=1)
    is_live = jnp.any(hit_mask, axis=1).astype(jnp.int32)
    slot_index = jnp.where(is_live == 1, jnp.cumsum(is_live, axis=0) - 1, -1)
    placing = slot_index[:, :, None] == jnp.arange(capacity, dtype=jnp.int32)[None, None, :]
    panels = jnp.einsum(
        "tqc,td->qcd", placing.astype(jnp.bfloat16), tokens, preferred_element_type=jnp.float32
    ).astype(jnp.bfloat16)

    def outer_xor(v, s):
        return lax.ppermute(v, "outer", [(i, i ^ s) for i in range(n_out)])

    def local_xor(v, m):
        return lax.ppermute(v, "local", [(i, i ^ m) for i in range(n_loc)])

    def both_xor(v, s, m):
        if s == 0 and m == 0:
            return v
        pairs = [(a * n_loc + b, (a ^ s) * n_loc + (b ^ m)) for a in range(n_out) for b in range(n_loc)]
        return lax.ppermute(v, ("outer", "local"), pairs)

    group = max(1, n_out // 4)
    chunks = [list(range(g, g + group)) for g in range(0, n_out, group)]
    pieces = {}
    for steps in chunks:
        mine = jnp.stack([panels[s] if s == 0 else outer_xor(panels[s], s) for s in steps])
        blocks = [None] * n_loc
        for m in range(0, n_loc, 2):
            blocks[m] = mine if m == 0 else local_xor(mine, m)
        for m in range(0, n_loc, 2):
            blocks[m + 1] = local_xor(blocks[m], 1)
        rows = jnp.stack(blocks).reshape(-1, width)
        gate_proj = jnp.dot(rows, gate_local, preferred_element_type=jnp.float32)
        up_proj = jnp.dot(rows, up_local, preferred_element_type=jnp.float32)
        hidden = (jax.nn.silu(gate_proj) * up_proj).astype(jnp.bfloat16)
        parts = [hidden if m == 0 else local_xor(hidden, m) for m in range(n_loc)]
        parts = [v.reshape(n_loc, -1, part_hid) for v in parts]
        full = jnp.concatenate(
            [jnp.concatenate([parts[m][j ^ m] for m in range(n_loc)], axis=1) for j in range(n_loc)], axis=0
        )
        expert_out = jnp.dot(full, down_local, preferred_element_type=jnp.float32).astype(jnp.bfloat16)
        expert_out = expert_out.reshape(n_loc, len(steps), capacity, part_out)
        for at, s in enumerate(steps):
            for m in range(n_loc):
                pieces[s, m] = both_xor(expert_out[m, at], s, m)

    spread = jnp.where(placing, fixed[:, :, None], 0).reshape(tok_rows, -1)
    high = (spread >> 8).astype(jnp.bfloat16)
    low = (spread & 255).astype(jnp.bfloat16)
    combined = jnp.zeros((tok_rows, width), jnp.float32)
    for m in range(n_loc):
        returned = jnp.concatenate([pieces[s, m] for s in range(n_out)], axis=0)
        block = jnp.dot(high, returned, preferred_element_type=jnp.float32) * (1.0 / 256.0)
        block += jnp.dot(low, returned, preferred_element_type=jnp.float32) * (1.0 / 65536.0)
        combined = lax.dynamic_update_slice(combined, block, (0, (l ^ m) * part_out))
    return combined


def solution(mesh):
    in_specs = (
        P(("groups", "outer", "local"), None),
        P(("groups", "outer", "local"), None),
        P(("groups", "outer", "local"), None),
        P("outer", None, "local"),
        P("outer", None, "local"),
        P("outer", None, "local"),
    )
    out_specs = P(("groups", "outer", "local"), None)
    return jax.shard_map(
        per_device, mesh=mesh, in_specs=in_specs, out_specs=out_specs, check_vma=False
    )
```

```python
import jax
import jax.numpy as jnp
from jax import lax
from jax.sharding import PartitionSpec as P

EXP_POD = 8


def per_device(tokens, routes, combine_fixed, gate_weight, up_weight, down_weight):
    tok_rows, width = tokens.shape
    n_out = lax.axis_size("outer")
    n_loc = lax.axis_size("local")
    n_chip = n_loc // 2
    capacity = 3 * tok_rows // (2 * n_out)
    part_out = down_weight.shape[2]
    part_hid = gate_weight.shape[2]
    z = lax.axis_index("outer")
    l = lax.axis_index("local")
    gate_local = gate_weight[0]
    up_local = up_weight[0]

    def down_rows(core):
        return jnp.concatenate(
            [
                lax.dynamic_slice_in_dim(down_weight[0], (l ^ (2 * x + core)) * part_hid, part_hid, 0)
                for x in range(n_chip)
            ],
            axis=0,
        )

    down_same, down_other = down_rows(0), down_rows(1)

    targets = (z ^ jnp.arange(n_out, dtype=jnp.int32)) * EXP_POD
    hit_mask = routes[:, :, None] == targets[None, None, :]
    fixed = jnp.sum(jnp.where(hit_mask, combine_fixed[:, :, None], 0), axis=1)
    is_live = jnp.any(hit_mask, axis=1).astype(jnp.int32)
    slot_index = jnp.where(is_live == 1, jnp.cumsum(is_live, axis=0) - 1, -1)
    placing = slot_index[:, :, None] == jnp.arange(capacity, dtype=jnp.int32)[None, None, :]
    panels = jnp.einsum(
        "tqc,td->qcd", placing.astype(jnp.bfloat16), tokens, preferred_element_type=jnp.float32
    ).astype(jnp.bfloat16)

    def outer_xor(v, s):
        return lax.ppermute(v, "outer", [(i, i ^ s) for i in range(n_out)])

    def local_xor(v, m):
        return lax.ppermute(v, "local", [(i, i ^ m) for i in range(n_loc)])

    def both_xor(v, s, m):
        if s == 0 and m == 0:
            return v
        pairs = [(a * n_loc + b, (a ^ s) * n_loc + (b ^ m)) for a in range(n_out) for b in range(n_loc)]
        return lax.ppermute(v, ("outer", "local"), pairs)

    half = n_out // 2
    pieces = {}
    for steps in (list(range(half)), list(range(half, n_out))):
        count = len(steps)
        mine = {s: panels[s] if s == 0 else outer_xor(panels[s], s) for s in steps}
        rows_same = jnp.concatenate(
            [mine[s] if x == 0 else local_xor(mine[s], 2 * x) for x in range(n_chip) for s in steps], axis=0
        )
        rows_other = local_xor(rows_same, 1)

        def first_half(rows):
            gate_proj = jnp.dot(rows, gate_local, preferred_element_type=jnp.float32)
            up_proj = jnp.dot(rows, up_local, preferred_element_type=jnp.float32)
            return (jax.nn.silu(gate_proj) * up_proj).astype(jnp.bfloat16)

        hidden = jnp.concatenate([first_half(rows_same), first_half(rows_other)], axis=0)
        sides = []
        for x in range(n_chip):
            side = hidden if x == 0 else local_xor(hidden, 2 * x)
            side = side.reshape(2, n_chip, -1, part_hid)
            sides.append(jnp.concatenate([side[:, y ^ x : (y ^ x) + 1] for y in range(n_chip)], axis=1))
        hidden_same = jnp.concatenate(sides, axis=3).reshape(2 * n_chip * count * capacity, n_chip * part_hid)
        hidden_other = local_xor(hidden_same, 1)
        out_same = jnp.dot(hidden_same, down_same, preferred_element_type=jnp.float32)
        out_other = jnp.dot(hidden_other, down_other, preferred_element_type=jnp.float32)
        out_other = out_other.reshape(2, -1, part_out)
        out_other = jnp.concatenate([out_other[1:], out_other[:1]], axis=0).reshape(out_same.shape)
        expert_out = (out_same + out_other).astype(jnp.bfloat16)
        expert_out = expert_out.reshape(2, n_chip, count, capacity, part_out)
        landed = {
            (at, x): both_xor(expert_out[:, x, at], s, 2 * x) for at, s in enumerate(steps) for x in range(n_chip)
        }
        swapped = local_xor(
            jnp.stack([landed[at, x][1] for at in range(count) for x in range(n_chip)]), 1
        )
        for at, s in enumerate(steps):
            for x in range(n_chip):
                pieces[s, 2 * x] = landed[at, x][0]
                pieces[s, 2 * x + 1] = swapped[at * n_chip + x]

    spread = jnp.where(placing, fixed[:, :, None], 0).reshape(tok_rows, -1)
    high = (spread >> 8).astype(jnp.bfloat16)
    low = (spread & 255).astype(jnp.bfloat16)
    combined = jnp.zeros((tok_rows, width), jnp.float32)
    for m in range(n_loc):
        returned = jnp.concatenate([pieces[s, m] for s in range(n_out)], axis=0)
        block = jnp.dot(high, returned, preferred_element_type=jnp.float32) * (1.0 / 256.0)
        block += jnp.dot(low, returned, preferred_element_type=jnp.float32) * (1.0 / 65536.0)
        combined = lax.dynamic_update_slice(combined, block, (0, (l ^ m) * part_out))
    return combined


def solution(mesh):
    in_specs = (
        P(("groups", "outer", "local"), None),
        P(("groups", "outer", "local"), None),
        P(("groups", "outer", "local"), None),
        P("outer", None, "local"),
        P("outer", None, "local"),
        P("outer", None, "local"),
    )
    out_specs = P(("groups", "outer", "local"), None)
    return jax.shard_map(
        per_device, mesh=mesh, in_specs=in_specs, out_specs=out_specs, check_vma=False
    )
```

```python
import jax
import jax.numpy as jnp
from jax import lax
from jax.sharding import PartitionSpec as P

EXP_POD = 8


def after(value, *earlier):
    return lax.optimization_barrier((value,) + earlier)[0]


def per_device(tokens, routes, combine_fixed, gate_weight, up_weight, down_weight):
    tok_rows, width = tokens.shape
    n_out = lax.axis_size("outer")
    n_loc = lax.axis_size("local")
    n_chip = n_loc // 2
    capacity = 3 * tok_rows // (2 * n_out)
    part_out = down_weight.shape[2]
    part_hid = gate_weight.shape[2]
    z = lax.axis_index("outer")
    l = lax.axis_index("local")
    gate_local = gate_weight[0]
    up_local = up_weight[0]

    def down_rows(core):
        return jnp.concatenate(
            [
                lax.dynamic_slice_in_dim(down_weight[0], (l ^ (2 * x + core)) * part_hid, part_hid, 0)
                for x in range(n_chip)
            ],
            axis=0,
        )

    down_same, down_other = down_rows(0), down_rows(1)

    targets = (z ^ jnp.arange(n_out, dtype=jnp.int32)) * EXP_POD
    hit_mask = routes[:, :, None] == targets[None, None, :]
    fixed = jnp.sum(jnp.where(hit_mask, combine_fixed[:, :, None], 0), axis=1)
    is_live = jnp.any(hit_mask, axis=1).astype(jnp.int32)
    slot_index = jnp.where(is_live == 1, jnp.cumsum(is_live, axis=0) - 1, -1)
    placing = slot_index[:, :, None] == jnp.arange(capacity, dtype=jnp.int32)[None, None, :]
    panels = jnp.einsum(
        "tqc,td->qcd", placing.astype(jnp.bfloat16), tokens, preferred_element_type=jnp.float32
    ).astype(jnp.bfloat16)

    def outer_xor(v, s):
        return lax.ppermute(v, "outer", [(i, i ^ s) for i in range(n_out)])

    def local_xor(v, m):
        return lax.ppermute(v, "local", [(i, i ^ m) for i in range(n_loc)])

    def both_xor(v, s, m):
        if s == 0 and m == 0:
            return v
        pairs = [(a * n_loc + b, (a ^ s) * n_loc + (b ^ m)) for a in range(n_out) for b in range(n_loc)]
        return lax.ppermute(v, ("outer", "local"), pairs)

    def first_half(rows):
        gate_proj = jnp.dot(rows, gate_local, preferred_element_type=jnp.float32)
        up_proj = jnp.dot(rows, up_local, preferred_element_type=jnp.float32)
        return (jax.nn.silu(gate_proj) * up_proj).astype(jnp.bfloat16)

    quarter = max(1, n_out // 4)
    near = list(range(n_out - 2 * quarter))
    far = list(range(n_out - quarter, n_out))
    mid = list(range(n_out - 2 * quarter, n_out - quarter))

    mine = {0: panels[0]}
    chip_of = {}

    def to_chips(steps):
        for s in steps:
            chip_of[s, 0] = mine[s]
            for x in range(1, n_chip):
                chip_of[s, x] = local_xor(mine[s], 2 * x)

    for s in near[1:] + far:
        mine[s] = outer_xor(panels[s], s)
    to_chips(near)
    for s in mid:
        mine[s] = outer_xor(after(panels[s], mine[near[-1]]), s)
    for s in far:
        mine[s] = after(mine[s], chip_of[near[-1], n_chip - 1])
    to_chips(far)
    for s in mid:
        mine[s] = after(mine[s], chip_of[far[-1], n_chip - 1])
    to_chips(mid)

    pieces = {}
    landed = {}
    for steps in (near, far, mid):
        count = len(steps)
        pairs = []
        for x in range(n_chip):
            if steps is mid and x > 0:
                for s in steps:
                    chip_of[s, x] = after(chip_of[s, x], hidden_other)
            same = jnp.concatenate([chip_of[s, x] for s in steps], axis=0)
            pairs.append(first_half(jnp.concatenate([same, local_xor(same, 1)], axis=0)))
        hidden = jnp.concatenate(pairs, axis=0)
        sides = []
        for x in range(n_chip):
            side = hidden if x == 0 else local_xor(hidden, 2 * x)
            side = side.reshape(n_chip, -1, part_hid)
            sides.append(jnp.concatenate([side[y ^ x : (y ^ x) + 1] for y in range(n_chip)], axis=0))
        hidden_same = jnp.concatenate(sides, axis=2).reshape(2 * n_chip * count * capacity, n_chip * part_hid)
        hidden_other = local_xor(hidden_same, 1)
        out_same = jnp.dot(hidden_same, down_same, preferred_element_type=jnp.float32)
        out_other = jnp.dot(hidden_other, down_other, preferred_element_type=jnp.float32)
        out_other = out_other.reshape(n_chip, 2, -1, part_out)
        out_other = jnp.concatenate([out_other[:, 1:], out_other[:, :1]], axis=1).reshape(out_same.shape)
        expert_out = (out_same + out_other).astype(jnp.bfloat16)
        expert_out = expert_out.reshape(n_chip, 2, count, capacity, part_out)
        if steps is near:
            for x in range(n_chip):
                block = expert_out[x] if x == 0 else local_xor(expert_out[x], 2 * x)
                for at, s in enumerate(steps):
                    landed[s, x] = block[:, at]
            for s in steps[1:]:
                moved = outer_xor(jnp.stack([landed[s, x] for x in range(n_chip)]), s)
                for x in range(n_chip):
                    landed[s, x] = moved[x]
        else:
            for at, s in enumerate(steps):
                for x in range(n_chip):
                    landed[s, x] = both_xor(expert_out[x, :, at], s, 2 * x)

    for steps in (far + near, mid):
        for s in steps:
            for x in range(n_chip):
                landed[s, x] = after(landed[s, x], swapped if steps is mid else expert_out)
        swapped = local_xor(jnp.stack([landed[s, x][1] for s in steps for x in range(n_chip)]), 1)
        for at, s in enumerate(steps):
            for x in range(n_chip):
                pieces[s, 2 * x] = landed[s, x][0]
                pieces[s, 2 * x + 1] = swapped[at * n_chip + x]

    spread = jnp.where(placing, fixed[:, :, None], 0).reshape(tok_rows, -1)
    high = (spread >> 8).astype(jnp.bfloat16)
    low = (spread & 255).astype(jnp.bfloat16)
    combined = jnp.zeros((tok_rows, width), jnp.float32)
    for m in range(n_loc):
        returned = jnp.concatenate([pieces[s, m] for s in range(n_out)], axis=0)
        block = jnp.dot(high, returned, preferred_element_type=jnp.float32) * (1.0 / 256.0)
        block += jnp.dot(low, returned, preferred_element_type=jnp.float32) * (1.0 / 65536.0)
        combined = lax.dynamic_update_slice(combined, block, (0, (l ^ m) * part_out))
    return combined


def solution(mesh):
    in_specs = (
        P(("groups", "outer", "local"), None),
        P(("groups", "outer", "local"), None),
        P(("groups", "outer", "local"), None),
        P("outer", None, "local"),
        P("outer", None, "local"),
        P("outer", None, "local"),
    )
    out_specs = P(("groups", "outer", "local"), None)
    return jax.shard_map(
        per_device, mesh=mesh, in_specs=in_specs, out_specs=out_specs, check_vma=False
    )
```

```python
import jax
import jax.numpy as jnp
from jax import lax
from jax.sharding import PartitionSpec as P

EXP_POD = 8


def after(value, *earlier):
    return lax.optimization_barrier((value,) + earlier)[0]


def per_device(tokens, routes, combine_fixed, gate_weight, up_weight, down_weight):
    tok_rows, width = tokens.shape
    n_out = lax.axis_size("outer")
    n_loc = lax.axis_size("local")
    n_chip = n_loc // 2
    capacity = 3 * tok_rows // (2 * n_out)
    part_out = down_weight.shape[2]
    part_hid = gate_weight.shape[2]
    z = lax.axis_index("outer")
    l = lax.axis_index("local")
    gate_local = gate_weight[0]
    up_local = up_weight[0]

    def down_rows(core):
        return jnp.concatenate(
            [
                lax.dynamic_slice_in_dim(down_weight[0], (l ^ (2 * x + core)) * part_hid, part_hid, 0)
                for x in range(n_chip)
            ],
            axis=0,
        )

    down_same, down_other = down_rows(0), down_rows(1)

    targets = (z ^ jnp.arange(n_out, dtype=jnp.int32)) * EXP_POD
    hit_mask = routes[:, :, None] == targets[None, None, :]
    fixed = jnp.sum(jnp.where(hit_mask, combine_fixed[:, :, None], 0), axis=1)
    is_live = jnp.any(hit_mask, axis=1).astype(jnp.int32)
    slot_index = jnp.where(is_live == 1, jnp.cumsum(is_live, axis=0) - 1, -1)
    placing = slot_index[:, :, None] == jnp.arange(capacity, dtype=jnp.int32)[None, None, :]
    panels = jnp.einsum(
        "tqc,td->qcd", placing.astype(jnp.bfloat16), tokens, preferred_element_type=jnp.float32
    ).astype(jnp.bfloat16)

    def outer_xor(v, s):
        return lax.ppermute(v, "outer", [(i, i ^ s) for i in range(n_out)])

    def local_xor(v, m):
        return lax.ppermute(v, "local", [(i, i ^ m) for i in range(n_loc)])

    def both_xor(v, s, m):
        if s == 0 and m == 0:
            return v
        pairs = [(a * n_loc + b, (a ^ s) * n_loc + (b ^ m)) for a in range(n_out) for b in range(n_loc)]
        return lax.ppermute(v, ("outer", "local"), pairs)

    def first_half(rows):
        gate_proj = jnp.dot(rows, gate_local, preferred_element_type=jnp.float32)
        up_proj = jnp.dot(rows, up_local, preferred_element_type=jnp.float32)
        return (jax.nn.silu(gate_proj) * up_proj).astype(jnp.bfloat16)

    quarter = max(1, n_out // 4)
    near = list(range(n_out - 2 * quarter))
    far = list(range(n_out - quarter, n_out))
    mid = list(range(n_out - 2 * quarter, n_out - quarter))

    mine = {0: panels[0]}
    chip_of = {}
    hidden_of = {}
    landed = {}
    pieces = {}

    def to_chips(steps):
        for s in steps:
            chip_of[s, 0] = mine[s]
            for x in range(1, n_chip):
                chip_of[s, x] = local_xor(mine[s], 2 * x)

    def make_hidden(steps):
        same = jnp.concatenate([chip_of[s, x] for x in range(n_chip) for s in steps], axis=0)
        other = local_xor(same, 1)
        halves = [first_half(rows).reshape(n_chip, -1, part_hid) for rows in (same, other)]
        return jnp.stack(halves, axis=1).reshape(-1, part_hid)

    def make_out(hidden, count):
        sides = []
        for x in range(n_chip):
            side = hidden if x == 0 else local_xor(hidden, 2 * x)
            side = side.reshape(n_chip, -1, part_hid)
            sides.append(jnp.concatenate([side[y ^ x : (y ^ x) + 1] for y in range(n_chip)], axis=0))
        hidden_same = jnp.concatenate(sides, axis=2).reshape(2 * n_chip * count * capacity, n_chip * part_hid)
        hidden_other = local_xor(hidden_same, 1)
        out_same = jnp.dot(hidden_same, down_same, preferred_element_type=jnp.float32)
        out_other = jnp.dot(hidden_other, down_other, preferred_element_type=jnp.float32)
        out_other = out_other.reshape(n_chip, 2, -1, part_out)
        out_other = jnp.concatenate([out_other[:, 1:], out_other[:, :1]], axis=1).reshape(out_same.shape)
        expert_out = (out_same + out_other).astype(jnp.bfloat16)
        return expert_out.reshape(n_chip, 2, count, capacity, part_out), hidden_other

    for s in far + near[1:] + mid:
        mine[s] = outer_xor(panels[s], s)
    chip_of[0, 0] = after(mine[0], mine[far[-1]])
    for x in range(1, n_chip):
        chip_of[0, x] = after(local_xor(mine[0], 2 * x), mine[far[-1]])
    for s in near[1:]:
        mine[s] = after(mine[s], mine[far[-1]])
    to_chips(near[1:])
    to_chips(far)
    for s in mid:
        mine[s] = after(mine[s], chip_of[near[-1], n_chip - 1])
    to_chips(mid)
    hidden_near = make_hidden(near)
    out_near, seen = make_out(hidden_near, len(near))
    for x in range(1, n_chip):
        for s in mid:
            chip_of[s, x] = after(chip_of[s, x], seen)
    hidden_far = make_hidden(far + mid)
    out_far, seen = make_out(hidden_far, len(far + mid))
    for at, s in enumerate(far + mid):
        for x in range(n_chip):
            landed[s, x] = both_xor(out_far[x, :, at], s, 2 * x)
    for x in range(n_chip):
        block = out_near[x] if x == 0 else local_xor(after(out_near[x], hidden_far), 2 * x)
        for at, s in enumerate(near):
            landed[s, x] = block[:, at]
    for s in near[1:]:
        sent = jnp.stack([landed[s, x] for x in range(n_chip)])
        moved = outer_xor(after(sent, out_far), s)
        for x in range(n_chip):
            landed[s, x] = moved[x]
    swapped = local_xor(jnp.stack([landed[s, x][1] for s in range(n_out) for x in range(n_chip)]), 1)
    for s in range(n_out):
        for x in range(n_chip):
            pieces[s, 2 * x] = landed[s, x][0]
            pieces[s, 2 * x + 1] = swapped[s * n_chip + x]

    spread = jnp.where(placing, fixed[:, :, None], 0).reshape(tok_rows, -1)
    high = (spread >> 8).astype(jnp.bfloat16)
    low = (spread & 255).astype(jnp.bfloat16)
    combined = jnp.zeros((tok_rows, width), jnp.float32)
    for m in range(n_loc):
        returned = jnp.concatenate([pieces[s, m] for s in range(n_out)], axis=0)
        block = jnp.dot(high, returned, preferred_element_type=jnp.float32) * (1.0 / 256.0)
        block += jnp.dot(low, returned, preferred_element_type=jnp.float32) * (1.0 / 65536.0)
        combined = lax.dynamic_update_slice(combined, block, (0, (l ^ m) * part_out))
    return combined


def solution(mesh):
    in_specs = (
        P(("groups", "outer", "local"), None),
        P(("groups", "outer", "local"), None),
        P(("groups", "outer", "local"), None),
        P("outer", None, "local"),
        P("outer", None, "local"),
        P("outer", None, "local"),
    )
    out_specs = P(("groups", "outer", "local"), None)
    return jax.shard_map(
        per_device, mesh=mesh, in_specs=in_specs, out_specs=out_specs, check_vma=False
    )
```

```python
import jax
import jax.numpy as jnp
from jax import lax
from jax.experimental import pallas as pl
from jax.experimental.pallas import tpu as pltpu
from jax.sharding import PartitionSpec as P
import functools

EXP_POD = 8
CFG = {'C': [[0, 3], [1, 2]], 'H': [[0], [1]], 'order': [['z', 0], ['x', [0]], ['z', 2], ['x', [2]], ['z', 3], ['x', [3]], ['z', 1], ['x', [1]], ['c', 1], ['h', 1], ['r', 2], ['c', 0], ['h', 0], ['r', 3], ['t', [0, 1]], ['w', [0, 1, 2, 3]]], 'gates': {'rs31': ['xd01'], 'rs20': ['zd2'], 'xs21': ['zd2'], 'cs1': ['zd3', 'xd01'], 'td01': ['xd01']}}


def sort_kernel(n_out, capacity, pods, tokens, routes, fixed, *outs):
    tok_rows = tokens.shape[0]
    rows = lax.broadcasted_iota(jnp.int32, (tok_rows, tok_rows), 0)
    cols = lax.broadcasted_iota(jnp.int32, (tok_rows, tok_rows), 1)
    upto = jnp.where(rows <= cols, 1.0, 0.0).astype(jnp.bfloat16)
    slot_of = lax.broadcasted_iota(jnp.int32, (capacity, tok_rows), 0)
    live, share = [], []
    for s in range(n_out):
        hit = routes[...] == pods[s]
        live.append(jnp.sum(jnp.where(hit, 1.0, 0.0), axis=0, keepdims=True))
        share.append(jnp.sum(jnp.where(hit, fixed[...], 0), axis=0, keepdims=True))
    flags = jnp.concatenate(live + [jnp.zeros((8 - n_out % 8, tok_rows), jnp.float32)] if n_out % 8 else live, axis=0)
    count = jnp.dot(flags.astype(jnp.bfloat16), upto, preferred_element_type=jnp.float32)
    place = []
    for s in range(n_out):
        slot = jnp.where(live[s] > 0.0, count[s : s + 1].astype(jnp.int32) - 1, -1)
        here = slot_of == slot
        place.append(jnp.where(here, 1.0, 0.0))
        spread = jnp.where(here, share[s], 0)
        outs[n_out][s] = (spread >> 8).astype(jnp.float32).astype(jnp.bfloat16)
        outs[n_out + 1][s] = (spread & 255).astype(jnp.float32).astype(jnp.bfloat16)
    chosen = jnp.concatenate(place, axis=0).astype(jnp.bfloat16)
    panels = jnp.dot(chosen, tokens[...], preferred_element_type=jnp.float32)
    for s in range(n_out):
        outs[s][...] = panels[s * capacity : (s + 1) * capacity].astype(jnp.bfloat16)

def sort_call(tokens, routes, fixed, pods, n_out, capacity):
    tok_rows, width = tokens.shape
    vmem = pl.BlockSpec(memory_space=pltpu.VMEM)
    outs = [jax.ShapeDtypeStruct((capacity, width), jnp.bfloat16)] * n_out
    outs += [jax.ShapeDtypeStruct((n_out, capacity, tok_rows), jnp.bfloat16)] * 2
    return pl.pallas_call(
        functools.partial(sort_kernel, n_out, capacity),
        in_specs=[pl.BlockSpec(memory_space=pltpu.SMEM), vmem, vmem, vmem],
        out_specs=[vmem] * len(outs), out_shape=outs,
        compiler_params=pltpu.CompilerParams(vmem_limit_bytes=16 * 1024 * 1024),
        name="pick_rows",
    )(pods, tokens, routes.T, fixed.T)

def combine_kernel(n_out, n_chip, groups, cols, weights, *refs):
    landed, swaps, out = refs[: n_out * n_chip], refs[n_out * n_chip : -1], refs[-1]
    tok_rows = out.shape[0]

    def rows_of(s, x, core):
        if not core:
            return landed[s * n_chip + x][0]
        for at, steps in enumerate(groups):
            if s in steps:
                return swaps[at][steps.index(s) * n_chip + x]

    for m in range(2 * n_chip):

        @pl.when(pl.program_id(0) == m)
        def _(m=m):
            parts = [rows_of(s, m // 2, m % 2).astype(jnp.float32) for s in range(n_out)]
            rows = jnp.concatenate(parts, axis=0).astype(jnp.bfloat16)
            both = jnp.dot(weights[...], rows, preferred_element_type=jnp.float32)
            out[...] = both[:tok_rows] * (1.0 / 256.0) + both[tok_rows:] * (1.0 / 65536.0)


def combine_call(weights, landed, swaps, cols, n_out, n_chip, capacity, tok_rows):
    arrived = [landed[s, x] for s in range(n_out) for x in range(n_chip)]
    groups = [tuple(steps) for steps, _ in swaps]
    traded = [v for _, v in swaps]
    part_out = traded[0].shape[-1]
    n_loc = 2 * n_chip
    spec_l = pl.BlockSpec((1, capacity, part_out), lambda m, cols: (0, 0, 0))
    return pl.pallas_call(
        functools.partial(combine_kernel, n_out, n_chip, groups),
        grid_spec=pltpu.PrefetchScalarGridSpec(
            num_scalar_prefetch=1,
            grid=(n_loc,),
            in_specs=[pl.BlockSpec(weights.shape, lambda m, cols: (0, 0))]
            + [spec_l] * len(arrived)
            + [pl.BlockSpec(v.shape, lambda m, cols: (0, 0, 0)) for v in traded],
            out_specs=pl.BlockSpec((tok_rows, part_out), lambda m, cols: (0, cols[m])),
        ),
        out_shape=jax.ShapeDtypeStruct((tok_rows, n_loc * part_out), jnp.float32),
        compiler_params=pltpu.CompilerParams(vmem_limit_bytes=16 * 1024 * 1024),
        name="weigh_rows",
    )(cols, weights, *arrived, *traded)


def per_device(tokens, routes, combine_fixed, gate_weight, up_weight, down_weight):
    tok_rows, width = tokens.shape
    n_out = lax.axis_size("outer")
    n_loc = lax.axis_size("local")
    n_chip = n_loc // 2
    capacity = 3 * tok_rows // (2 * n_out)
    part_out = down_weight.shape[2]
    part_hid = gate_weight.shape[2]
    z = lax.axis_index("outer")
    l = lax.axis_index("local")
    gate_local = gate_weight[0]
    up_local = up_weight[0]
    seen = {}
    gates = CFG["gates"]

    def gated(name, value):
        names = [g for g in gates.get(name, ()) if g in seen]
        if names:
            value = lax.optimization_barrier((value,) + tuple(seen[g] for g in names))[0]
        seen[name] = value
        return value

    def down_rows(core):
        return jnp.concatenate(
            [
                lax.dynamic_slice_in_dim(down_weight[0], (l ^ (2 * x + core)) * part_hid, part_hid, 0)
                for x in range(n_chip)
            ],
            axis=0,
        )

    down_same, down_other = down_rows(0), down_rows(1)
    pods = (z ^ jnp.arange(n_out, dtype=jnp.int32)) * EXP_POD
    in_kernels = n_out == 4 and capacity % 8 == 0 and part_out % 128 == 0
    if in_kernels:
        *panels, high, low = sort_call(tokens, routes, combine_fixed, pods, n_out, capacity)
        high = high.reshape(-1, tok_rows).T
        low = low.reshape(-1, tok_rows).T
    else:
        hit_mask = routes[:, :, None] == pods[None, None, :]
        fixed = jnp.sum(jnp.where(hit_mask, combine_fixed[:, :, None], 0), axis=1)
        is_live = jnp.any(hit_mask, axis=1).astype(jnp.int32)
        slot_index = jnp.where(is_live == 1, jnp.cumsum(is_live, axis=0) - 1, -1)
        placing = slot_index[:, :, None] == jnp.arange(capacity, dtype=jnp.int32)[None, None, :]
        panels = jnp.einsum(
            "tqc,td->qcd", placing.astype(jnp.bfloat16), tokens, preferred_element_type=jnp.float32
        ).astype(jnp.bfloat16)
        panels = panels.reshape(4, -1, width)
        spread = jnp.where(placing, fixed[:, :, None], 0).reshape(tok_rows, -1)
        high = (spread >> 8).astype(jnp.bfloat16)
        low = (spread & 255).astype(jnp.bfloat16)

    span = n_out // 4

    def by_pod(v, s, axis, move):
        if span == 1:
            return move(v, s) if s else v
        parts = jnp.split(v, span, axis=axis)
        parts = [move(p, s * span + i) if s * span + i else p for i, p in enumerate(parts)]
        return jnp.concatenate(parts, axis=axis)

    def outer_xor(v, s, axis):
        return by_pod(v, s, axis, lambda p, t: lax.ppermute(p, "outer", [(i, i ^ t) for i in range(n_out)]))

    def local_xor(v, m):
        return lax.ppermute(v, "local", [(i, i ^ m) for i in range(n_loc)])

    def both_xor(v, s, m):
        if m == 0:
            return outer_xor(v, s, 1)

        def move(p, t):
            pairs = [(a * n_loc + b, (a ^ t) * n_loc + (b ^ m)) for a in range(n_out) for b in range(n_loc)]
            return lax.ppermute(p, ("outer", "local"), pairs)

        if span == 1:
            return move(v, s)
        parts = jnp.split(v, span, axis=1)
        return jnp.concatenate([move(p, s * span + i) for i, p in enumerate(parts)], axis=1)

    def first_half(rows):
        gate_proj = jnp.dot(rows, gate_local, preferred_element_type=jnp.float32)
        up_proj = jnp.dot(rows, up_local, preferred_element_type=jnp.float32)
        return (jax.nn.silu(gate_proj) * up_proj).astype(jnp.bfloat16)

    chip_of = {}
    hid = []
    outs = {}
    landed = {}
    pieces = {}
    swaps = []
    mine = {}
    todo = list(CFG["order"])
    for item in todo:
        kind, arg = item
        if kind == "z":
            s = arg
            mine[s] = gated(f"zd{s}", outer_xor(gated(f"zs{s}", panels[s]), s, 0))
        elif kind == "x":
            for s in arg:
                chip_of[s, 0] = mine[s]
            for x in range(1, n_chip):
                held = [mine[s] for s in arg]
                held = held[0] if len(arg) == 1 else jnp.stack(held)
                got = gated(f"xd{arg[0]}{x}", local_xor(gated(f"xs{arg[0]}{x}", held), 2 * x))
                for at, s in enumerate(arg):
                    chip_of[s, x] = got if len(arg) == 1 else got[at]
        elif kind == "c":
            steps = CFG["C"][arg]
            same = jnp.concatenate([chip_of[s, x] for x in range(n_chip) for s in steps], axis=0)
            other = gated(f"cd{arg}", local_xor(gated(f"cs{arg}", same), 1))
            halves = [first_half(rows).reshape(n_chip, -1, part_hid) for rows in (same, other)]
            hid.append((arg, jnp.stack(halves, axis=1)))
        elif kind == "h":
            cs = CFG["H"][arg]
            steps = [s for c in cs for s in CFG["C"][c]]
            count = len(steps)
            hd = dict(hid)
            hidden = jnp.concatenate([hd[c] for c in cs], axis=2)
            hidden = gated(f"hs{arg}", hidden)
            sides = []
            for x in range(n_chip):
                side = hidden if x == 0 else gated(f"hd{arg}{x}", local_xor(hidden, 2 * x))
                sides.append(jnp.concatenate([side[y ^ x : (y ^ x) + 1] for y in range(n_chip)], axis=0))
            hidden_same = jnp.concatenate(sides, axis=3).reshape(2 * n_chip * count * span * capacity, n_chip * part_hid)
            hidden_other = gated(f"kd{arg}", local_xor(gated(f"ks{arg}", hidden_same), 1))
            out_same = jnp.dot(hidden_same, down_same, preferred_element_type=jnp.float32)
            out_other = jnp.dot(hidden_other, down_other, preferred_element_type=jnp.float32)
            out_other = out_other.reshape(n_chip, 2, -1, part_out)
            out_other = jnp.concatenate([out_other[:, 1:], out_other[:, :1]], axis=1).reshape(out_same.shape)
            expert_out = (out_same + out_other).astype(jnp.bfloat16)
            expert_out = expert_out.reshape(n_chip, 2, count, span * capacity, part_out)
            for at, s in enumerate(steps):
                outs[s] = expert_out[:, :, at]
        elif kind == "r":
            s = arg
            for x in range(n_chip):
                landed[s, x] = gated(f"rd{s}{x}", both_xor(gated(f"rs{s}{x}", outs[s][x]), s, 2 * x))
        elif kind == "t":
            for x in range(n_chip):
                block = jnp.stack([outs[s][x] for s in arg], axis=1)
                if x:
                    block = gated(f"td{arg[0]}{x}", local_xor(gated(f"ts{arg[0]}{x}", block), 2 * x))
                for at, s in enumerate(arg):
                    landed[s, x] = block[:, at]
            for s in arg:
                if s or span > 1:
                    moved = outer_xor(gated(f"rs{s}0", jnp.stack([landed[s, x] for x in range(n_chip)])), s, 2)
                    moved = gated(f"rd{s}0", moved)
                    for x in range(n_chip):
                        landed[s, x] = moved[x]
        elif kind == "w":
            steps = arg
            stack = gated(f"ws{steps[0]}", jnp.stack([landed[s, x][1] for s in steps for x in range(n_chip)]))
            swapped = gated(f"wd{steps[0]}", local_xor(stack, 1))
            for at, s in enumerate(steps):
                for x in range(n_chip):
                    pieces[s, 2 * x] = landed[s, x][0]
                    pieces[s, 2 * x + 1] = swapped[at * n_chip + x]
            swaps.append((steps, swapped))

    if in_kernels:
        cols = l ^ jnp.arange(n_loc, dtype=jnp.int32)
        weights = jnp.concatenate([high, low], axis=0)
        return combine_call(weights, landed, swaps, cols, n_out, n_chip, capacity, tok_rows)
    combined = jnp.zeros((tok_rows, width), jnp.float32)
    for m in range(n_loc):
        returned = jnp.concatenate([pieces[s, m] for s in range(4)], axis=0)
        block = jnp.dot(high, returned, preferred_element_type=jnp.float32) * (1.0 / 256.0)
        block += jnp.dot(low, returned, preferred_element_type=jnp.float32) * (1.0 / 65536.0)
        combined = lax.dynamic_update_slice(combined, block, (0, (l ^ m) * part_out))
    return combined


def solution(mesh):
    in_specs = (
        P(("groups", "outer", "local"), None),
        P(("groups", "outer", "local"), None),
        P(("groups", "outer", "local"), None),
        P("outer", None, "local"),
        P("outer", None, "local"),
        P("outer", None, "local"),
    )
    out_specs = P(("groups", "outer", "local"), None)
    return jax.shard_map(
        per_device, mesh=mesh, in_specs=in_specs, out_specs=out_specs, check_vma=False
    )
```

```python
import jax
import jax.numpy as jnp
from jax import lax
from jax.experimental import pallas as pl
from jax.experimental.pallas import tpu as pltpu
from jax.sharding import PartitionSpec as P
import functools

EXP_POD = 8
CFG = {'C': [[0, 3], [1, 2]], 'H': [[0], [1]], 'order': [['z', 3], ['x', [3]], ['z', 2], ['x', [2]], ['z', 0], ['z', 1], ['x', [1]], ['x', [0]], ['c', 1], ['h', 1], ['r', 2], ['c', 0], ['h', 0], ['r', 3], ['t', [0, 1]], ['w', [0, 1, 2, 3]]], 'gates': {'rs31': ['xd01'], 'rs20': ['zd2'], 'cs1': ['zd3', 'xd01'], 'td01': ['xd01'], 'rd30': ['hd11']}, 'apart': False}


def pick_kernel(n_out, capacity, pods, tokens_hbm, routes_hbm, fixed_hbm, *refs):
    panels, (high, low) = refs[:n_out], refs[n_out : n_out + 2]
    tokens, routes, fixed, sems = refs[n_out + 2 :]
    copies = [
        pltpu.make_async_copy(src, dst, sems.at[i])
        for i, (src, dst) in enumerate(((routes_hbm, routes), (fixed_hbm, fixed), (tokens_hbm, tokens)))
    ]
    for copy in copies:
        copy.start()
    tok_rows = tokens.shape[0]
    rows = lax.broadcasted_iota(jnp.int32, (tok_rows, tok_rows), 0)
    cols = lax.broadcasted_iota(jnp.int32, (tok_rows, tok_rows), 1)
    upto = jnp.where(rows <= cols, 1.0, 0.0).astype(jnp.bfloat16)
    slot_of = lax.broadcasted_iota(jnp.int32, (capacity, tok_rows), 0)
    copies[0].wait()
    hits = [routes[...] == pods[s] for s in range(n_out)]
    live = [jnp.sum(jnp.where(hit, 1.0, 0.0), axis=0, keepdims=True) for hit in hits]
    spare = [jnp.zeros((8 - n_out, tok_rows), jnp.float32)]
    count = jnp.dot(jnp.concatenate(live + spare, axis=0).astype(jnp.bfloat16), upto, preferred_element_type=jnp.float32)
    here = []
    for s in range(n_out):
        slot = jnp.where(live[s] > 0.0, count[s : s + 1].astype(jnp.int32) - 1, -1)
        here.append(slot_of == slot)
    chosen = jnp.concatenate([jnp.where(h, 1.0, 0.0) for h in here], axis=0).astype(jnp.bfloat16)
    copies[2].wait()
    picked = jnp.dot(chosen, tokens[...], preferred_element_type=jnp.float32)
    for s in range(n_out):
        panels[s][...] = picked[s * capacity : (s + 1) * capacity].astype(jnp.bfloat16)
    copies[1].wait()
    for s in range(n_out):
        share = jnp.sum(jnp.where(hits[s], fixed[...], 0), axis=0, keepdims=True)
        spread = jnp.where(here[s], share, 0)
        high[s] = (spread >> 8).astype(jnp.float32)
        low[s] = (spread & 255).astype(jnp.float32)


def pick_call(tokens, routes, fixed, pods, n_out, capacity):
    tok_rows, width = tokens.shape
    vmem = pl.BlockSpec(memory_space=pltpu.VMEM)
    away = pl.BlockSpec(memory_space=pl.ANY)
    outs = [jax.ShapeDtypeStruct((capacity, width), jnp.bfloat16)] * n_out
    outs += [jax.ShapeDtypeStruct((n_out, capacity, tok_rows), jnp.float32)] * 2
    return pl.pallas_call(
        functools.partial(pick_kernel, n_out, capacity),
        in_specs=[pl.BlockSpec(memory_space=pltpu.SMEM), away, away, away],
        out_specs=[vmem] * len(outs),
        out_shape=outs,
        scratch_shapes=[
            pltpu.VMEM(tokens.shape, tokens.dtype),
            pltpu.VMEM(routes.shape[::-1], routes.dtype),
            pltpu.VMEM(fixed.shape[::-1], fixed.dtype),
            pltpu.SemaphoreType.DMA((3,)),
        ],
        compiler_params=pltpu.CompilerParams(vmem_limit_bytes=56 * 1024 * 1024),
        name="pick_rows",
    )(pods, tokens, routes.T, fixed.T)


def combine_kernel(n_out, n_chip, groups, cols, weights, *refs):
    n_in = n_out * n_chip
    landed, traded, out = refs[:n_in], refs[n_in : n_in + len(groups)], refs[n_in + len(groups)]
    own, other, sums, sems, out_sems = refs[n_in + len(groups) + 1 :]
    tok_rows, part_out = sums.shape[1:]
    own_copies = [pltpu.make_async_copy(landed[i].at[0], own.at[i], sems.at[i]) for i in range(n_in)]
    other_copies, first = [], 0
    for i, ref in enumerate(traded):
        count = ref.shape[0]
        other_copies.append(pltpu.make_async_copy(ref, other.at[pl.ds(first, count)], sems.at[n_in + i]))
        first += count
    for copy in own_copies + other_copies:
        copy.start()
    order = [s for steps in groups for s in steps]
    finals = []
    for core in range(2):
        for copy in (own_copies, other_copies)[core]:
            copy.wait()
        for x in range(n_chip):
            if core:
                parts = [other[order.index(s) * n_chip + x] for s in range(n_out)]
            else:
                parts = [own[s * n_chip + x] for s in range(n_out)]
            rows = jnp.concatenate([p.astype(jnp.float32) for p in parts], axis=0).astype(jnp.bfloat16)
            both = jnp.dot(weights[...], rows, preferred_element_type=jnp.float32)
            m = 2 * x + core
            sums[m] = both[:tok_rows] * (1.0 / 256.0) + both[tok_rows:] * (1.0 / 65536.0)
            columns = pl.ds(pl.multiple_of(cols[m] * part_out, 128), part_out)
            finals.append(pltpu.make_async_copy(sums.at[m], out.at[:, columns], out_sems.at[m]))
            finals[-1].start()
    for copy in finals:
        copy.wait()


def combine_call(weights, landed, swaps, cols, n_out, n_chip, capacity, tok_rows):
    arrived = [landed[s, x] for s in range(n_out) for x in range(n_chip)]
    groups = [tuple(steps) for steps, _ in swaps]
    traded = [v for _, v in swaps]
    part_out = traded[0].shape[-1]
    n_loc = 2 * n_chip
    away = pl.BlockSpec(memory_space=pl.ANY)
    return pl.pallas_call(
        functools.partial(combine_kernel, n_out, n_chip, groups),
        in_specs=[pl.BlockSpec(memory_space=pltpu.SMEM), pl.BlockSpec(memory_space=pltpu.VMEM)]
        + [away] * (len(arrived) + len(traded)),
        out_specs=away,
        out_shape=jax.ShapeDtypeStruct((tok_rows, n_loc * part_out), jnp.float32),
        scratch_shapes=[
            pltpu.VMEM((n_out * n_chip, capacity, part_out), jnp.bfloat16),
            pltpu.VMEM((n_out * n_chip, capacity, part_out), jnp.bfloat16),
            pltpu.VMEM((n_loc, tok_rows, part_out), jnp.float32),
            pltpu.SemaphoreType.DMA((len(arrived) + len(traded),)),
            pltpu.SemaphoreType.DMA((n_loc,)),
        ],
        compiler_params=pltpu.CompilerParams(vmem_limit_bytes=16 * 1024 * 1024),
        name="weigh_rows",
    )(cols, weights, *arrived, *traded)


def per_device(tokens, routes, combine_fixed, gate_weight, up_weight, down_weight):
    tok_rows, width = tokens.shape
    n_out = lax.axis_size("outer")
    n_loc = lax.axis_size("local")
    n_chip = n_loc // 2
    capacity = 3 * tok_rows // (2 * n_out)
    part_out = down_weight.shape[2]
    part_hid = gate_weight.shape[2]
    z = lax.axis_index("outer")
    l = lax.axis_index("local")
    gate_local = gate_weight[0]
    up_local = up_weight[0]
    seen = {}
    gates = CFG["gates"]

    def gated(name, value):
        names = [g for g in gates.get(name, ()) if g in seen]
        if names:
            value = lax.optimization_barrier((value,) + tuple(seen[g] for g in names))[0]
        seen[name] = value
        return value

    def down_rows(core):
        return jnp.concatenate(
            [
                lax.dynamic_slice_in_dim(down_weight[0], (l ^ (2 * x + core)) * part_hid, part_hid, 0)
                for x in range(n_chip)
            ],
            axis=0,
        )

    down_same, down_other = down_rows(0), down_rows(1)
    pods = (z ^ jnp.arange(n_out, dtype=jnp.int32)) * EXP_POD
    in_kernels = n_out == 4 and capacity % 8 == 0 and part_out % 128 == 0
    if in_kernels:
        *panels, high, low = pick_call(tokens, routes, combine_fixed, pods, n_out, capacity)
        high = high.reshape(-1, tok_rows).T.astype(jnp.bfloat16)
        low = low.reshape(-1, tok_rows).T.astype(jnp.bfloat16)
    else:
        hit_mask = routes[:, :, None] == pods[None, None, :]
        fixed = jnp.sum(jnp.where(hit_mask, combine_fixed[:, :, None], 0), axis=1)
        is_live = jnp.any(hit_mask, axis=1).astype(jnp.int32)
        slot_index = jnp.where(is_live == 1, jnp.cumsum(is_live, axis=0) - 1, -1)
        placing = slot_index[:, :, None] == jnp.arange(capacity, dtype=jnp.int32)[None, None, :]
        panels = jnp.einsum(
            "tqc,td->qcd", placing.astype(jnp.bfloat16), tokens, preferred_element_type=jnp.float32
        ).astype(jnp.bfloat16)
        panels = panels.reshape(4, -1, width)
        spread = jnp.where(placing, fixed[:, :, None], 0).reshape(tok_rows, -1)
        high = (spread >> 8).astype(jnp.bfloat16)
        low = (spread & 255).astype(jnp.bfloat16)

    span = n_out // 4

    def by_pod(v, s, axis, move):
        if span == 1:
            return move(v, s) if s else v
        parts = jnp.split(v, span, axis=axis)
        parts = [move(p, s * span + i) if s * span + i else p for i, p in enumerate(parts)]
        return jnp.concatenate(parts, axis=axis)

    def outer_xor(v, s, axis):
        return by_pod(v, s, axis, lambda p, t: lax.ppermute(p, "outer", [(i, i ^ t) for i in range(n_out)]))

    def local_xor(v, m):
        return lax.ppermute(v, "local", [(i, i ^ m) for i in range(n_loc)])

    def both_xor(v, s, m):
        if m == 0:
            return outer_xor(v, s, 1)

        def move(p, t):
            pairs = [(a * n_loc + b, (a ^ t) * n_loc + (b ^ m)) for a in range(n_out) for b in range(n_loc)]
            return lax.ppermute(p, ("outer", "local"), pairs)

        if span == 1:
            return move(v, s)
        parts = jnp.split(v, span, axis=1)
        return jnp.concatenate([move(p, s * span + i) for i, p in enumerate(parts)], axis=1)

    def first_half(rows):
        gate_proj = jnp.dot(rows, gate_local, preferred_element_type=jnp.float32)
        up_proj = jnp.dot(rows, up_local, preferred_element_type=jnp.float32)
        return (jax.nn.silu(gate_proj) * up_proj).astype(jnp.bfloat16)

    chip_of = {}
    hid = []
    outs = {}
    landed = {}
    pieces = {}
    swaps = []
    mine = {}
    todo = list(CFG["order"])
    for item in todo:
        kind, arg = item
        if kind == "z":
            s = arg
            mine[s] = gated(f"zd{s}", outer_xor(gated(f"zs{s}", panels[s]), s, 0))
        elif kind == "x":
            for s in arg:
                chip_of[s, 0] = mine[s]
            for x in range(1, n_chip):
                held = [mine[s] for s in arg]
                held = held[0] if len(arg) == 1 else jnp.stack(held)
                got = gated(f"xd{arg[0]}{x}", local_xor(gated(f"xs{arg[0]}{x}", held), 2 * x))
                for at, s in enumerate(arg):
                    chip_of[s, x] = got if len(arg) == 1 else got[at]
        elif kind == "c":
            steps = CFG["C"][arg]
            if CFG["apart"]:
                sides = []
                for x in range(n_chip):
                    same = jnp.concatenate([chip_of[s, x] for s in steps], axis=0)
                    other = gated(f"cd{arg}{x}", local_xor(gated(f"cs{arg}{x}", same), 1))
                    sides.append(first_half(jnp.concatenate([same, other], axis=0)).reshape(2, -1, part_hid))
                hid.append((arg, jnp.stack(sides)))
            else:
                same = jnp.concatenate([chip_of[s, x] for x in range(n_chip) for s in steps], axis=0)
                other = gated(f"cd{arg}", local_xor(gated(f"cs{arg}", same), 1))
                halves = [first_half(rows).reshape(n_chip, -1, part_hid) for rows in (same, other)]
                hid.append((arg, jnp.stack(halves, axis=1)))
        elif kind == "h":
            cs = CFG["H"][arg]
            steps = [s for c in cs for s in CFG["C"][c]]
            count = len(steps)
            hd = dict(hid)
            hidden = jnp.concatenate([hd[c] for c in cs], axis=2)
            hidden = gated(f"hs{arg}", hidden)
            sides = []
            for x in range(n_chip):
                side = hidden if x == 0 else gated(f"hd{arg}{x}", local_xor(hidden, 2 * x))
                sides.append(jnp.concatenate([side[y ^ x : (y ^ x) + 1] for y in range(n_chip)], axis=0))
            hidden_same = jnp.concatenate(sides, axis=3).reshape(2 * n_chip * count * span * capacity, n_chip * part_hid)
            hidden_other = gated(f"kd{arg}", local_xor(gated(f"ks{arg}", hidden_same), 1))
            out_same = jnp.dot(hidden_same, down_same, preferred_element_type=jnp.float32)
            out_other = jnp.dot(hidden_other, down_other, preferred_element_type=jnp.float32)
            out_other = out_other.reshape(n_chip, 2, -1, part_out)
            out_other = jnp.concatenate([out_other[:, 1:], out_other[:, :1]], axis=1).reshape(out_same.shape)
            expert_out = (out_same + out_other).astype(jnp.bfloat16)
            expert_out = expert_out.reshape(n_chip, 2, count, span * capacity, part_out)
            for at, s in enumerate(steps):
                outs[s] = expert_out[:, :, at]
        elif kind == "r":
            s = arg
            for x in range(n_chip):
                landed[s, x] = gated(f"rd{s}{x}", both_xor(gated(f"rs{s}{x}", outs[s][x]), s, 2 * x))
        elif kind == "t":
            for x in range(n_chip):
                block = jnp.stack([outs[s][x] for s in arg], axis=1)
                if x:
                    block = gated(f"td{arg[0]}{x}", local_xor(gated(f"ts{arg[0]}{x}", block), 2 * x))
                for at, s in enumerate(arg):
                    landed[s, x] = block[:, at]
            for s in arg:
                if s or span > 1:
                    moved = outer_xor(gated(f"rs{s}0", jnp.stack([landed[s, x] for x in range(n_chip)])), s, 2)
                    moved = gated(f"rd{s}0", moved)
                    for x in range(n_chip):
                        landed[s, x] = moved[x]
        elif kind == "w":
            steps = arg
            stack = gated(f"ws{steps[0]}", jnp.stack([landed[s, x][1] for s in steps for x in range(n_chip)]))
            swapped = gated(f"wd{steps[0]}", local_xor(stack, 1))
            for at, s in enumerate(steps):
                for x in range(n_chip):
                    pieces[s, 2 * x] = landed[s, x][0]
                    pieces[s, 2 * x + 1] = swapped[at * n_chip + x]
            swaps.append((steps, swapped))

    if in_kernels:
        cols = l ^ jnp.arange(n_loc, dtype=jnp.int32)
        weights = jnp.concatenate([high, low], axis=0)
        return combine_call(weights, landed, swaps, cols, n_out, n_chip, capacity, tok_rows)
    combined = jnp.zeros((tok_rows, width), jnp.float32)
    for m in range(n_loc):
        returned = jnp.concatenate([pieces[s, m] for s in range(4)], axis=0)
        block = jnp.dot(high, returned, preferred_element_type=jnp.float32) * (1.0 / 256.0)
        block += jnp.dot(low, returned, preferred_element_type=jnp.float32) * (1.0 / 65536.0)
        combined = lax.dynamic_update_slice(combined, block, (0, (l ^ m) * part_out))
    return combined


def solution(mesh):
    in_specs = (
        P(("groups", "outer", "local"), None),
        P(("groups", "outer", "local"), None),
        P(("groups", "outer", "local"), None),
        P("outer", None, "local"),
        P("outer", None, "local"),
        P("outer", None, "local"),
    )
    out_specs = P(("groups", "outer", "local"), None)
    return jax.shard_map(
        per_device, mesh=mesh, in_specs=in_specs, out_specs=out_specs, check_vma=False
    )
```

```python
import jax
import jax.numpy as jnp
from jax import lax
from jax.experimental import pallas as pl
from jax.experimental.pallas import tpu as pltpu
from jax.sharding import PartitionSpec as P
import functools

EXP_POD = 8
CFG = {'C': [[0, 3], [1, 2]], 'H': [[0], [1]], 'order': [('z', 0), ('z', 3), ('z', 1), ('x', (0,)), ('z', 2), ('x', (3,)), ('c', 0), ('h', 0), ('x', (1,)), ('x', (2,)), ('c', 1), ('h', 1), ('q', (3, 0)), ('q', (2, 1)), ('v', ((3, 0), (2, 1)))], 'gates': {'qd3': ['xd11']}, 'apart': False}


def pick_kernel(n_out, capacity, pods, tokens_hbm, routes_hbm, fixed_hbm, *refs):
    panels, (high, low) = refs[:n_out], refs[n_out : n_out + 2]
    tokens, routes, fixed, sems = refs[n_out + 2 :]
    copies = [
        pltpu.make_async_copy(src, dst, sems.at[i])
        for i, (src, dst) in enumerate(((routes_hbm, routes), (fixed_hbm, fixed), (tokens_hbm, tokens)))
    ]
    for copy in copies:
        copy.start()
    tok_rows = tokens.shape[0]
    rows = lax.broadcasted_iota(jnp.int32, (tok_rows, tok_rows), 0)
    cols = lax.broadcasted_iota(jnp.int32, (tok_rows, tok_rows), 1)
    upto = jnp.where(rows <= cols, 1.0, 0.0).astype(jnp.bfloat16)
    slot_of = lax.broadcasted_iota(jnp.int32, (capacity, tok_rows), 0)
    copies[0].wait()
    hits = [routes[...] == pods[s] for s in range(n_out)]
    live = [jnp.sum(jnp.where(hit, 1.0, 0.0), axis=0, keepdims=True) for hit in hits]
    spare = [jnp.zeros((8 - n_out, tok_rows), jnp.float32)]
    count = jnp.dot(jnp.concatenate(live + spare, axis=0).astype(jnp.bfloat16), upto, preferred_element_type=jnp.float32)
    here = []
    for s in range(n_out):
        slot = jnp.where(live[s] > 0.0, count[s : s + 1].astype(jnp.int32) - 1, -1)
        here.append(slot_of == slot)
    chosen = jnp.concatenate([jnp.where(h, 1.0, 0.0) for h in here], axis=0).astype(jnp.bfloat16)
    copies[2].wait()
    picked = jnp.dot(chosen, tokens[...], preferred_element_type=jnp.float32)
    for s in range(n_out):
        panels[s][...] = picked[s * capacity : (s + 1) * capacity].astype(jnp.bfloat16)
    copies[1].wait()
    for s in range(n_out):
        share = jnp.sum(jnp.where(hits[s], fixed[...], 0), axis=0, keepdims=True)
        spread = jnp.where(here[s], share, 0)
        high[s] = (spread >> 8).astype(jnp.float32)
        low[s] = (spread & 255).astype(jnp.float32)


def pick_call(tokens, routes, fixed, pods, n_out, capacity):
    tok_rows, width = tokens.shape
    vmem = pl.BlockSpec(memory_space=pltpu.VMEM)
    away = pl.BlockSpec(memory_space=pl.ANY)
    outs = [jax.ShapeDtypeStruct((capacity, width), jnp.bfloat16)] * n_out
    outs += [jax.ShapeDtypeStruct((n_out, capacity, tok_rows), jnp.float32)] * 2
    return pl.pallas_call(
        functools.partial(pick_kernel, n_out, capacity),
        in_specs=[pl.BlockSpec(memory_space=pltpu.SMEM), away, away, away],
        out_specs=[vmem] * len(outs),
        out_shape=outs,
        scratch_shapes=[
            pltpu.VMEM(tokens.shape, tokens.dtype),
            pltpu.VMEM(routes.shape[::-1], routes.dtype),
            pltpu.VMEM(fixed.shape[::-1], fixed.dtype),
            pltpu.SemaphoreType.DMA((3,)),
        ],
        compiler_params=pltpu.CompilerParams(vmem_limit_bytes=56 * 1024 * 1024),
        name="pick_rows",
    )(pods, tokens, routes.T, fixed.T)


def combine_kernel(n_out, n_chip, groups, cols, weights, *refs):
    n_in = n_out * n_chip
    landed, traded, out = refs[:n_in], refs[n_in : n_in + len(groups)], refs[n_in + len(groups)]
    own, other, sums, sems, out_sems = refs[n_in + len(groups) + 1 :]
    tok_rows, part_out = sums.shape[1:]
    own_copies = [pltpu.make_async_copy(landed[i].at[0], own.at[i], sems.at[i]) for i in range(n_in)]
    other_copies, first = [], 0
    for i, ref in enumerate(traded):
        count = ref.shape[0]
        other_copies.append(pltpu.make_async_copy(ref, other.at[pl.ds(first, count)], sems.at[n_in + i]))
        first += count
    for copy in own_copies + other_copies:
        copy.start()
    order = [s for steps in groups for s in steps]
    finals = []
    for core in range(2):
        for copy in (own_copies, other_copies)[core]:
            copy.wait()
        for x in range(n_chip):
            if core:
                parts = [other[order.index(s) * n_chip + x] for s in range(n_out)]
            else:
                parts = [own[s * n_chip + x] for s in range(n_out)]
            rows = jnp.concatenate([p.astype(jnp.float32) for p in parts], axis=0).astype(jnp.bfloat16)
            both = jnp.dot(weights[...], rows, preferred_element_type=jnp.float32)
            m = 2 * x + core
            sums[m] = both[:tok_rows] * (1.0 / 256.0) + both[tok_rows:] * (1.0 / 65536.0)
            columns = pl.ds(pl.multiple_of(cols[m] * part_out, 128), part_out)
            finals.append(pltpu.make_async_copy(sums.at[m], out.at[:, columns], out_sems.at[m]))
            finals[-1].start()
    for copy in finals:
        copy.wait()


def combine_call(weights, landed, swaps, cols, n_out, n_chip, capacity, tok_rows):
    arrived = [landed[s, x] for s in range(n_out) for x in range(n_chip)]
    groups = [tuple(steps) for steps, _ in swaps]
    traded = [v for _, v in swaps]
    part_out = traded[0].shape[-1]
    n_loc = 2 * n_chip
    away = pl.BlockSpec(memory_space=pl.ANY)
    return pl.pallas_call(
        functools.partial(combine_kernel, n_out, n_chip, groups),
        in_specs=[pl.BlockSpec(memory_space=pltpu.SMEM), pl.BlockSpec(memory_space=pltpu.VMEM)]
        + [away] * (len(arrived) + len(traded)),
        out_specs=away,
        out_shape=jax.ShapeDtypeStruct((tok_rows, n_loc * part_out), jnp.float32),
        scratch_shapes=[
            pltpu.VMEM((n_out * n_chip, capacity, part_out), jnp.bfloat16),
            pltpu.VMEM((n_out * n_chip, capacity, part_out), jnp.bfloat16),
            pltpu.VMEM((n_loc, tok_rows, part_out), jnp.float32),
            pltpu.SemaphoreType.DMA((len(arrived) + len(traded),)),
            pltpu.SemaphoreType.DMA((n_loc,)),
        ],
        compiler_params=pltpu.CompilerParams(vmem_limit_bytes=16 * 1024 * 1024),
        name="weigh_rows",
    )(cols, weights, *arrived, *traded)


def per_device(tokens, routes, combine_fixed, gate_weight, up_weight, down_weight):
    tok_rows, width = tokens.shape
    n_out = lax.axis_size("outer")
    n_loc = lax.axis_size("local")
    n_chip = n_loc // 2
    capacity = 3 * tok_rows // (2 * n_out)
    part_out = down_weight.shape[2]
    part_hid = gate_weight.shape[2]
    z = lax.axis_index("outer")
    l = lax.axis_index("local")
    gate_local = gate_weight[0]
    up_local = up_weight[0]
    seen = {}
    gates = CFG["gates"]

    def gated(name, value):
        names = [g for g in gates.get(name, ()) if g in seen]
        if names:
            value = lax.optimization_barrier((value,) + tuple(seen[g] for g in names))[0]
        seen[name] = value
        return value

    def down_rows(core):
        return jnp.concatenate(
            [
                lax.dynamic_slice_in_dim(down_weight[0], (l ^ (2 * x + core)) * part_hid, part_hid, 0)
                for x in range(n_chip)
            ],
            axis=0,
        )

    down_same, down_other = down_rows(0), down_rows(1)
    pods = (z ^ jnp.arange(n_out, dtype=jnp.int32)) * EXP_POD
    in_kernels = False and capacity % 8 == 0 and part_out % 128 == 0
    if in_kernels:
        *panels, high, low = pick_call(tokens, routes, combine_fixed, pods, n_out, capacity)
        high = high.reshape(-1, tok_rows).T.astype(jnp.bfloat16)
        low = low.reshape(-1, tok_rows).T.astype(jnp.bfloat16)
    else:
        hit_mask = routes[:, :, None] == pods[None, None, :]
        fixed = jnp.sum(jnp.where(hit_mask, combine_fixed[:, :, None], 0), axis=1)
        is_live = jnp.any(hit_mask, axis=1).astype(jnp.int32)
        slot_index = jnp.where(is_live == 1, jnp.cumsum(is_live, axis=0) - 1, -1)
        placing = slot_index[:, :, None] == jnp.arange(capacity, dtype=jnp.int32)[None, None, :]
        panels = jnp.einsum(
            "tqc,td->qcd", placing.astype(jnp.bfloat16), tokens, preferred_element_type=jnp.float32
        ).astype(jnp.bfloat16)
        panels = panels.reshape(4, -1, width)
        spread = jnp.where(placing, fixed[:, :, None], 0).reshape(tok_rows, -1)
        high = (spread >> 8).astype(jnp.bfloat16)
        low = (spread & 255).astype(jnp.bfloat16)

    span = n_out // 4

    def by_pod(v, s, axis, move):
        if span == 1:
            return move(v, s) if s else v
        parts = jnp.split(v, span, axis=axis)
        parts = [move(p, s * span + i) if s * span + i else p for i, p in enumerate(parts)]
        return jnp.concatenate(parts, axis=axis)

    def outer_xor(v, s, axis):
        return by_pod(v, s, axis, lambda p, t: lax.ppermute(p, "outer", [(i, i ^ t) for i in range(n_out)]))

    def local_xor(v, m):
        return lax.ppermute(v, "local", [(i, i ^ m) for i in range(n_loc)])

    def both_xor(v, s, m):
        if m == 0:
            return outer_xor(v, s, 1)

        def move(p, t):
            pairs = [(a * n_loc + b, (a ^ t) * n_loc + (b ^ m)) for a in range(n_out) for b in range(n_loc)]
            return lax.ppermute(p, ("outer", "local"), pairs)

        if span == 1:
            return move(v, s)
        parts = jnp.split(v, span, axis=1)
        return jnp.concatenate([move(p, s * span + i) for i, p in enumerate(parts)], axis=1)

    def first_half(rows):
        gate_proj = jnp.dot(rows, gate_local, preferred_element_type=jnp.float32)
        up_proj = jnp.dot(rows, up_local, preferred_element_type=jnp.float32)
        return (jax.nn.silu(gate_proj) * up_proj).astype(jnp.bfloat16)

    chip_of = {}
    hid = []
    outs = {}
    landed = {}
    pieces = {}
    back = {}
    shared = []
    swaps = []
    mine = {}
    todo = list(CFG["order"])
    for item in todo:
        kind, arg = item
        if kind == "z":
            s = arg
            mine[s] = gated(f"zd{s}", outer_xor(gated(f"zs{s}", panels[s]), s, 0))
        elif kind == "x":
            for s in arg:
                chip_of[s, 0] = mine[s]
            for x in range(1, n_chip):
                held = [mine[s] for s in arg]
                held = held[0] if len(arg) == 1 else jnp.stack(held)
                got = gated(f"xd{arg[0]}{x}", local_xor(gated(f"xs{arg[0]}{x}", held), 2 * x))
                for at, s in enumerate(arg):
                    chip_of[s, x] = got if len(arg) == 1 else got[at]
        elif kind == "c":
            steps = CFG["C"][arg]
            if CFG["apart"]:
                sides = []
                for x in range(n_chip):
                    same = jnp.concatenate([chip_of[s, x] for s in steps], axis=0)
                    other = gated(f"cd{arg}{x}", local_xor(gated(f"cs{arg}{x}", same), 1))
                    sides.append(first_half(jnp.concatenate([same, other], axis=0)).reshape(2, -1, part_hid))
                hid.append((arg, jnp.stack(sides)))
            else:
                same = jnp.concatenate([chip_of[s, x] for x in range(n_chip) for s in steps], axis=0)
                other = gated(f"cd{arg}", local_xor(gated(f"cs{arg}", same), 1))
                halves = [first_half(rows).reshape(n_chip, -1, part_hid) for rows in (same, other)]
                hid.append((arg, jnp.stack(halves, axis=1)))
        elif kind == "h":
            cs = CFG["H"][arg]
            steps = [s for c in cs for s in CFG["C"][c]]
            count = len(steps)
            hd = dict(hid)
            hidden = jnp.concatenate([hd[c] for c in cs], axis=2)
            hidden = gated(f"hs{arg}", hidden)
            sides = []
            for x in range(n_chip):
                side = hidden if x == 0 else gated(f"hd{arg}{x}", local_xor(hidden, 2 * x))
                sides.append(jnp.concatenate([side[y ^ x : (y ^ x) + 1] for y in range(n_chip)], axis=0))
            hidden_same = jnp.concatenate(sides, axis=3).reshape(2 * n_chip * count * span * capacity, n_chip * part_hid)
            hidden_other = gated(f"kd{arg}", local_xor(gated(f"ks{arg}", hidden_same), 1))
            out_same = jnp.dot(hidden_same, down_same, preferred_element_type=jnp.float32)
            out_other = jnp.dot(hidden_other, down_other, preferred_element_type=jnp.float32)
            out_other = out_other.reshape(n_chip, 2, -1, part_out)
            out_other = jnp.concatenate([out_other[:, 1:], out_other[:, :1]], axis=1).reshape(out_same.shape)
            expert_out = (out_same + out_other).astype(jnp.bfloat16)
            expert_out = expert_out.reshape(n_chip, 2, count, span * capacity, part_out)
            for at, s in enumerate(steps):
                outs[s] = expert_out[:, :, at]
        elif kind == "r":
            s = arg
            for x in range(n_chip):
                landed[s, x] = gated(f"rd{s}{x}", both_xor(gated(f"rs{s}{x}", outs[s][x]), s, 2 * x))
        elif kind == "t":
            for x in range(n_chip):
                block = jnp.stack([outs[s][x] for s in arg], axis=1)
                if x:
                    block = gated(f"td{arg[0]}{x}", local_xor(gated(f"ts{arg[0]}{x}", block), 2 * x))
                for at, s in enumerate(arg):
                    landed[s, x] = block[:, at]
            for s in arg:
                if s or span > 1:
                    moved = outer_xor(gated(f"rs{s}0", jnp.stack([landed[s, x] for x in range(n_chip)])), s, 2)
                    moved = gated(f"rd{s}0", moved)
                    for x in range(n_chip):
                        landed[s, x] = moved[x]
        elif kind == "q":
            a, b = arg
            core = l & 1
            kept = jnp.where(core == 0, outs[a], outs[b])
            given = gated(f"qs{a}", jnp.where(core == 0, outs[b], outs[a])[:, ::-1])
            taken = gated(f"qd{a}", local_xor(given, 1))
            for x in range(n_chip):
                block = gated(f"us{a}{x}", jnp.stack([kept[x], taken[x]]))

                def move(p, i, x=x):
                    pairs = []
                    for zz in range(n_out):
                        for ll in range(n_loc):
                            t = (b if ll & 1 else a) * span + i
                            pairs.append((zz * n_loc + ll, (zz ^ t) * n_loc + (ll ^ (2 * x))))
                    return lax.ppermute(p, ("outer", "local"), pairs)

                parts = [move(p, i) for i, p in enumerate(jnp.split(block, span, axis=2) if span > 1 else [block])]
                back[a, x] = gated(f"ud{a}{x}", parts[0] if span == 1 else jnp.concatenate(parts, axis=2))
        elif kind == "v":
            stack = jnp.stack([back[a, x][:, 1] for a, b in arg for x in range(n_chip)])
            swapped = gated(f"wd{arg[0][0]}", local_xor(gated(f"ws{arg[0][0]}", stack), 1))
            for at, (a, b) in enumerate(arg):
                for x in range(n_chip):
                    pieces[a, 2 * x] = back[a, x][0, 0]
                    pieces[a, 2 * x + 1] = back[a, x][1, 0]
                    pieces[b, 2 * x] = swapped[at * n_chip + x, 1]
                    pieces[b, 2 * x + 1] = swapped[at * n_chip + x, 0]
                shared.append((a, b))
        elif kind == "w":
            steps = arg
            stack = gated(f"ws{steps[0]}", jnp.stack([landed[s, x][1] for s in steps for x in range(n_chip)]))
            swapped = gated(f"wd{steps[0]}", local_xor(stack, 1))
            for at, s in enumerate(steps):
                for x in range(n_chip):
                    pieces[s, 2 * x] = landed[s, x][0]
                    pieces[s, 2 * x + 1] = swapped[at * n_chip + x]
            swaps.append((steps, swapped))

    if in_kernels:
        cols = l ^ jnp.arange(n_loc, dtype=jnp.int32)
        weights = jnp.concatenate([high, low], axis=0)
        return combine_call(weights, landed, swaps, cols, n_out, n_chip, capacity, tok_rows)
    def in_turn(w):
        cuts = jnp.split(w, 4, axis=1)
        for a, b in shared:
            cuts[a], cuts[b] = (jnp.where((l & 1) == 0, cuts[i], cuts[j]) for i, j in ((a, b), (b, a)))
        return jnp.concatenate(cuts, axis=1)

    high, low = in_turn(high), in_turn(low)
    combined = jnp.zeros((tok_rows, width), jnp.float32)
    for m in range(n_loc):
        returned = jnp.concatenate([pieces[s, m] for s in range(4)], axis=0)
        block = jnp.dot(high, returned, preferred_element_type=jnp.float32) * (1.0 / 256.0)
        block += jnp.dot(low, returned, preferred_element_type=jnp.float32) * (1.0 / 65536.0)
        combined = lax.dynamic_update_slice(combined, block, (0, (l ^ m) * part_out))
    return combined


def solution(mesh):
    in_specs = (
        P(("groups", "outer", "local"), None),
        P(("groups", "outer", "local"), None),
        P(("groups", "outer", "local"), None),
        P("outer", None, "local"),
        P("outer", None, "local"),
        P("outer", None, "local"),
    )
    out_specs = P(("groups", "outer", "local"), None)
    return jax.shard_map(
        per_device, mesh=mesh, in_specs=in_specs, out_specs=out_specs, check_vma=False
    )
```

```python
import jax
import jax.numpy as jnp
from jax import lax
from jax.experimental import pallas as pl
from jax.experimental.pallas import tpu as pltpu
from jax.sharding import PartitionSpec as P
import functools

EXP_POD = 8
CFG = {'C': [[0, 3], [1, 2]], 'H': [[0], [1]], 'order': [('z', 3), ('z', 1), ('x', (3,)), ('z', 2), ('x', (2,)), ('z', 0), ('x', (0,)), ('c', 0), ('h', 0), ('r', 3), ('x', (1,)), ('c', 1), ('h', 1), ('r', 2), ('t', (0, 1)), ('w', (0, 1, 2, 3))], 'gates': {'cs1': ['zd3', 'xd01'], 'td01': ['xd01'], 'rd30': ['hd11'], 'hs1': ['xd11'], 'rs31': ['cd0']}, 'apart': False}


def pick_kernel(n_out, capacity, pods, tokens_hbm, routes_hbm, fixed_hbm, *refs):
    panels, (high, low) = refs[:n_out], refs[n_out : n_out + 2]
    tokens, routes, fixed, sems = refs[n_out + 2 :]
    copies = [
        pltpu.make_async_copy(src, dst, sems.at[i])
        for i, (src, dst) in enumerate(((routes_hbm, routes), (fixed_hbm, fixed), (tokens_hbm, tokens)))
    ]
    for copy in copies:
        copy.start()
    tok_rows = tokens.shape[0]
    rows = lax.broadcasted_iota(jnp.int32, (tok_rows, tok_rows), 0)
    cols = lax.broadcasted_iota(jnp.int32, (tok_rows, tok_rows), 1)
    upto = jnp.where(rows <= cols, 1.0, 0.0).astype(jnp.bfloat16)
    slot_of = lax.broadcasted_iota(jnp.int32, (capacity, tok_rows), 0)
    copies[0].wait()
    hits = [routes[...] == pods[s] for s in range(n_out)]
    live = [jnp.sum(jnp.where(hit, 1.0, 0.0), axis=0, keepdims=True) for hit in hits]
    spare = [jnp.zeros((8 - n_out, tok_rows), jnp.float32)]
    count = jnp.dot(jnp.concatenate(live + spare, axis=0).astype(jnp.bfloat16), upto, preferred_element_type=jnp.float32)
    here = []
    for s in range(n_out):
        slot = jnp.where(live[s] > 0.0, count[s : s + 1].astype(jnp.int32) - 1, -1)
        here.append(slot_of == slot)
    chosen = jnp.concatenate([jnp.where(h, 1.0, 0.0) for h in here], axis=0).astype(jnp.bfloat16)
    copies[2].wait()
    picked = jnp.dot(chosen, tokens[...], preferred_element_type=jnp.float32)
    for s in range(n_out):
        panels[s][...] = picked[s * capacity : (s + 1) * capacity].astype(jnp.bfloat16)
    copies[1].wait()
    for s in range(n_out):
        share = jnp.sum(jnp.where(hits[s], fixed[...], 0), axis=0, keepdims=True)
        spread = jnp.where(here[s], share, 0)
        high[s] = (spread >> 8).astype(jnp.float32)
        low[s] = (spread & 255).astype(jnp.float32)


def pick_call(tokens, routes, fixed, pods, n_out, capacity):
    tok_rows, width = tokens.shape
    vmem = pl.BlockSpec(memory_space=pltpu.VMEM)
    away = pl.BlockSpec(memory_space=pl.ANY)
    outs = [jax.ShapeDtypeStruct((capacity, width), jnp.bfloat16)] * n_out
    outs += [jax.ShapeDtypeStruct((n_out, capacity, tok_rows), jnp.float32)] * 2
    return pl.pallas_call(
        functools.partial(pick_kernel, n_out, capacity),
        in_specs=[pl.BlockSpec(memory_space=pltpu.SMEM), away, away, away],
        out_specs=[vmem] * len(outs),
        out_shape=outs,
        scratch_shapes=[
            pltpu.VMEM(tokens.shape, tokens.dtype),
            pltpu.VMEM(routes.shape[::-1], routes.dtype),
            pltpu.VMEM(fixed.shape[::-1], fixed.dtype),
            pltpu.SemaphoreType.DMA((3,)),
        ],
        compiler_params=pltpu.CompilerParams(vmem_limit_bytes=56 * 1024 * 1024),
        name="pick_rows",
    )(pods, tokens, routes.T, fixed.T)


def combine_kernel(n_out, n_chip, groups, cols, weights, *refs):
    n_in = n_out * n_chip
    landed, traded, out = refs[:n_in], refs[n_in : n_in + len(groups)], refs[n_in + len(groups)]
    own, other, sums, sems, out_sems = refs[n_in + len(groups) + 1 :]
    tok_rows, part_out = sums.shape[1:]
    own_copies = [pltpu.make_async_copy(landed[i].at[0], own.at[i], sems.at[i]) for i in range(n_in)]
    other_copies, first = [], 0
    for i, ref in enumerate(traded):
        count = ref.shape[0]
        other_copies.append(pltpu.make_async_copy(ref, other.at[pl.ds(first, count)], sems.at[n_in + i]))
        first += count
    for copy in own_copies + other_copies:
        copy.start()
    order = [s for steps in groups for s in steps]
    finals = []
    for core in range(2):
        for copy in (own_copies, other_copies)[core]:
            copy.wait()
        for x in range(n_chip):
            if core:
                parts = [other[order.index(s) * n_chip + x] for s in range(n_out)]
            else:
                parts = [own[s * n_chip + x] for s in range(n_out)]
            rows = jnp.concatenate([p.astype(jnp.float32) for p in parts], axis=0).astype(jnp.bfloat16)
            both = jnp.dot(weights[...], rows, preferred_element_type=jnp.float32)
            m = 2 * x + core
            sums[m] = both[:tok_rows] * (1.0 / 256.0) + both[tok_rows:] * (1.0 / 65536.0)
            columns = pl.ds(pl.multiple_of(cols[m] * part_out, 128), part_out)
            finals.append(pltpu.make_async_copy(sums.at[m], out.at[:, columns], out_sems.at[m]))
            finals[-1].start()
    for copy in finals:
        copy.wait()


def combine_call(weights, landed, swaps, cols, n_out, n_chip, capacity, tok_rows):
    arrived = [landed[s, x] for s in range(n_out) for x in range(n_chip)]
    groups = [tuple(steps) for steps, _ in swaps]
    traded = [v for _, v in swaps]
    part_out = traded[0].shape[-1]
    n_loc = 2 * n_chip
    away = pl.BlockSpec(memory_space=pl.ANY)
    return pl.pallas_call(
        functools.partial(combine_kernel, n_out, n_chip, groups),
        in_specs=[pl.BlockSpec(memory_space=pltpu.SMEM), pl.BlockSpec(memory_space=pltpu.VMEM)]
        + [away] * (len(arrived) + len(traded)),
        out_specs=away,
        out_shape=jax.ShapeDtypeStruct((tok_rows, n_loc * part_out), jnp.float32),
        scratch_shapes=[
            pltpu.VMEM((n_out * n_chip, capacity, part_out), jnp.bfloat16),
            pltpu.VMEM((n_out * n_chip, capacity, part_out), jnp.bfloat16),
            pltpu.VMEM((n_loc, tok_rows, part_out), jnp.float32),
            pltpu.SemaphoreType.DMA((len(arrived) + len(traded),)),
            pltpu.SemaphoreType.DMA((n_loc,)),
        ],
        compiler_params=pltpu.CompilerParams(vmem_limit_bytes=16 * 1024 * 1024),
        name="weigh_rows",
    )(cols, weights, *arrived, *traded)


def per_device(tokens, routes, combine_fixed, gate_weight, up_weight, down_weight):
    tok_rows, width = tokens.shape
    n_out = lax.axis_size("outer")
    n_loc = lax.axis_size("local")
    n_chip = n_loc // 2
    capacity = 3 * tok_rows // (2 * n_out)
    part_out = down_weight.shape[2]
    part_hid = gate_weight.shape[2]
    z = lax.axis_index("outer")
    l = lax.axis_index("local")
    gate_local = gate_weight[0]
    up_local = up_weight[0]
    seen = {}
    gates = CFG["gates"]

    def gated(name, value):
        names = [g for g in gates.get(name, ()) if g in seen]
        if names:
            value = lax.optimization_barrier((value,) + tuple(seen[g] for g in names))[0]
        seen[name] = value
        return value

    def down_rows(core):
        return jnp.concatenate(
            [
                lax.dynamic_slice_in_dim(down_weight[0], (l ^ (2 * x + core)) * part_hid, part_hid, 0)
                for x in range(n_chip)
            ],
            axis=0,
        )

    down_same, down_other = down_rows(0), down_rows(1)
    pods = (z ^ jnp.arange(n_out, dtype=jnp.int32)) * EXP_POD
    in_kernels = False and capacity % 8 == 0 and part_out % 128 == 0
    if in_kernels:
        *panels, high, low = pick_call(tokens, routes, combine_fixed, pods, n_out, capacity)
        high = high.reshape(-1, tok_rows).T.astype(jnp.bfloat16)
        low = low.reshape(-1, tok_rows).T.astype(jnp.bfloat16)
    else:
        hit_mask = routes[:, :, None] == pods[None, None, :]
        fixed = jnp.sum(jnp.where(hit_mask, combine_fixed[:, :, None], 0), axis=1)
        is_live = jnp.any(hit_mask, axis=1).astype(jnp.int32)
        slot_index = jnp.where(is_live == 1, jnp.cumsum(is_live, axis=0) - 1, -1)
        placing = slot_index[:, :, None] == jnp.arange(capacity, dtype=jnp.int32)[None, None, :]
        panels = jnp.einsum(
            "tqc,td->qcd", placing.astype(jnp.bfloat16), tokens, preferred_element_type=jnp.float32
        ).astype(jnp.bfloat16)
        panels = panels.reshape(4, -1, width)
        spread = jnp.where(placing, fixed[:, :, None], 0).reshape(tok_rows, -1)
        high = (spread >> 8).astype(jnp.bfloat16)
        low = (spread & 255).astype(jnp.bfloat16)

    span = n_out // 4

    def by_pod(v, s, axis, move):
        if span == 1:
            return move(v, s) if s else v
        parts = jnp.split(v, span, axis=axis)
        parts = [move(p, s * span + i) if s * span + i else p for i, p in enumerate(parts)]
        return jnp.concatenate(parts, axis=axis)

    def outer_xor(v, s, axis):
        return by_pod(v, s, axis, lambda p, t: lax.ppermute(p, "outer", [(i, i ^ t) for i in range(n_out)]))

    def local_xor(v, m):
        return lax.ppermute(v, "local", [(i, i ^ m) for i in range(n_loc)])

    def both_xor(v, s, m):
        if m == 0:
            return outer_xor(v, s, 1)

        def move(p, t):
            pairs = [(a * n_loc + b, (a ^ t) * n_loc + (b ^ m)) for a in range(n_out) for b in range(n_loc)]
            return lax.ppermute(p, ("outer", "local"), pairs)

        if span == 1:
            return move(v, s)
        parts = jnp.split(v, span, axis=1)
        return jnp.concatenate([move(p, s * span + i) for i, p in enumerate(parts)], axis=1)

    def first_half(rows):
        gate_proj = jnp.dot(rows, gate_local, preferred_element_type=jnp.float32)
        up_proj = jnp.dot(rows, up_local, preferred_element_type=jnp.float32)
        return (jax.nn.silu(gate_proj) * up_proj).astype(jnp.bfloat16)

    chip_of = {}
    hid = []
    outs = {}
    landed = {}
    pieces = {}
    back = {}
    shared = []
    swaps = []
    mine = {}
    todo = list(CFG["order"])
    for item in todo:
        kind, arg = item
        if kind == "z":
            s = arg
            mine[s] = gated(f"zd{s}", outer_xor(gated(f"zs{s}", panels[s]), s, 0))
        elif kind == "x":
            for s in arg:
                chip_of[s, 0] = mine[s]
            for x in range(1, n_chip):
                held = [mine[s] for s in arg]
                held = held[0] if len(arg) == 1 else jnp.stack(held)
                got = gated(f"xd{arg[0]}{x}", local_xor(gated(f"xs{arg[0]}{x}", held), 2 * x))
                for at, s in enumerate(arg):
                    chip_of[s, x] = got if len(arg) == 1 else got[at]
        elif kind == "c":
            steps = CFG["C"][arg]
            if CFG["apart"]:
                sides = []
                for x in range(n_chip):
                    same = jnp.concatenate([chip_of[s, x] for s in steps], axis=0)
                    other = gated(f"cd{arg}{x}", local_xor(gated(f"cs{arg}{x}", same), 1))
                    sides.append(first_half(jnp.concatenate([same, other], axis=0)).reshape(2, -1, part_hid))
                hid.append((arg, jnp.stack(sides)))
            else:
                same = jnp.concatenate([chip_of[s, x] for x in range(n_chip) for s in steps], axis=0)
                other = gated(f"cd{arg}", local_xor(gated(f"cs{arg}", same), 1))
                halves = [first_half(rows).reshape(n_chip, -1, part_hid) for rows in (same, other)]
                hid.append((arg, jnp.stack(halves, axis=1)))
        elif kind == "h":
            cs = CFG["H"][arg]
            steps = [s for c in cs for s in CFG["C"][c]]
            count = len(steps)
            hd = dict(hid)
            hidden = jnp.concatenate([hd[c] for c in cs], axis=2)
            hidden = gated(f"hs{arg}", hidden)
            sides = []
            for x in range(n_chip):
                side = hidden if x == 0 else gated(f"hd{arg}{x}", local_xor(hidden, 2 * x))
                sides.append(jnp.concatenate([side[y ^ x : (y ^ x) + 1] for y in range(n_chip)], axis=0))
            hidden_same = jnp.concatenate(sides, axis=3).reshape(2 * n_chip * count * span * capacity, n_chip * part_hid)
            hidden_other = gated(f"kd{arg}", local_xor(gated(f"ks{arg}", hidden_same), 1))
            out_same = jnp.dot(hidden_same, down_same, preferred_element_type=jnp.float32)
            out_other = jnp.dot(hidden_other, down_other, preferred_element_type=jnp.float32)
            out_other = out_other.reshape(n_chip, 2, -1, part_out)
            out_other = jnp.concatenate([out_other[:, 1:], out_other[:, :1]], axis=1).reshape(out_same.shape)
            expert_out = (out_same + out_other).astype(jnp.bfloat16)
            expert_out = expert_out.reshape(n_chip, 2, count, span * capacity, part_out)
            for at, s in enumerate(steps):
                outs[s] = expert_out[:, :, at]
        elif kind == "r":
            s = arg
            for x in range(n_chip):
                landed[s, x] = gated(f"rd{s}{x}", both_xor(gated(f"rs{s}{x}", outs[s][x]), s, 2 * x))
        elif kind == "t":
            for x in range(n_chip):
                block = jnp.stack([outs[s][x] for s in arg], axis=1)
                if x:
                    block = gated(f"td{arg[0]}{x}", local_xor(gated(f"ts{arg[0]}{x}", block), 2 * x))
                for at, s in enumerate(arg):
                    landed[s, x] = block[:, at]
            for s in arg:
                if s or span > 1:
                    moved = outer_xor(gated(f"rs{s}0", jnp.stack([landed[s, x] for x in range(n_chip)])), s, 2)
                    moved = gated(f"rd{s}0", moved)
                    for x in range(n_chip):
                        landed[s, x] = moved[x]
        elif kind == "q":
            a, b = arg
            core = l & 1
            kept = jnp.where(core == 0, outs[a], outs[b])
            given = gated(f"qs{a}", jnp.where(core == 0, outs[b], outs[a])[:, ::-1])
            taken = gated(f"qd{a}", local_xor(given, 1))
            for x in range(n_chip):
                block = gated(f"us{a}{x}", jnp.stack([kept[x], taken[x]]))

                def move(p, i, x=x):
                    pairs = []
                    for zz in range(n_out):
                        for ll in range(n_loc):
                            t = (b if ll & 1 else a) * span + i
                            pairs.append((zz * n_loc + ll, (zz ^ t) * n_loc + (ll ^ (2 * x))))
                    return lax.ppermute(p, ("outer", "local"), pairs)

                parts = [move(p, i) for i, p in enumerate(jnp.split(block, span, axis=2) if span > 1 else [block])]
                back[a, x] = gated(f"ud{a}{x}", parts[0] if span == 1 else jnp.concatenate(parts, axis=2))
        elif kind == "v":
            stack = jnp.stack([back[a, x][:, 1] for a, b in arg for x in range(n_chip)])
            swapped = gated(f"wd{arg[0][0]}", local_xor(gated(f"ws{arg[0][0]}", stack), 1))
            for at, (a, b) in enumerate(arg):
                for x in range(n_chip):
                    pieces[a, 2 * x] = back[a, x][0, 0]
                    pieces[a, 2 * x + 1] = back[a, x][1, 0]
                    pieces[b, 2 * x] = swapped[at * n_chip + x, 1]
                    pieces[b, 2 * x + 1] = swapped[at * n_chip + x, 0]
                shared.append((a, b))
        elif kind == "w":
            steps = arg
            stack = gated(f"ws{steps[0]}", jnp.stack([landed[s, x][1] for s in steps for x in range(n_chip)]))
            swapped = gated(f"wd{steps[0]}", local_xor(stack, 1))
            for at, s in enumerate(steps):
                for x in range(n_chip):
                    pieces[s, 2 * x] = landed[s, x][0]
                    pieces[s, 2 * x + 1] = swapped[at * n_chip + x]
            swaps.append((steps, swapped))

    if in_kernels:
        cols = l ^ jnp.arange(n_loc, dtype=jnp.int32)
        weights = jnp.concatenate([high, low], axis=0)
        return combine_call(weights, landed, swaps, cols, n_out, n_chip, capacity, tok_rows)
    def in_turn(w):
        cuts = jnp.split(w, 4, axis=1)
        for a, b in shared:
            cuts[a], cuts[b] = (jnp.where((l & 1) == 0, cuts[i], cuts[j]) for i, j in ((a, b), (b, a)))
        return jnp.concatenate(cuts, axis=1)

    high, low = in_turn(high), in_turn(low)
    combined = jnp.zeros((tok_rows, width), jnp.float32)
    for m in range(n_loc):
        returned = jnp.concatenate([pieces[s, m] for s in range(4)], axis=0)
        block = jnp.dot(high, returned, preferred_element_type=jnp.float32) * (1.0 / 256.0)
        block += jnp.dot(low, returned, preferred_element_type=jnp.float32) * (1.0 / 65536.0)
        combined = lax.dynamic_update_slice(combined, block, (0, (l ^ m) * part_out))
    return combined


def solution(mesh):
    in_specs = (
        P(("groups", "outer", "local"), None),
        P(("groups", "outer", "local"), None),
        P(("groups", "outer", "local"), None),
        P("outer", None, "local"),
        P("outer", None, "local"),
        P("outer", None, "local"),
    )
    out_specs = P(("groups", "outer", "local"), None)
    return jax.shard_map(
        per_device, mesh=mesh, in_specs=in_specs, out_specs=out_specs, check_vma=False
    )
```

```python
import jax
import jax.numpy as jnp
from jax import lax
from jax.experimental import pallas as pl
from jax.experimental.pallas import tpu as pltpu
from jax.sharding import PartitionSpec as P
import functools

EXP_POD = 8
CFG = {'C': [[0, 3], [1, 2]], 'H': [[0], [1]], 'order': [('z', 0), ('z', 1), ('z', 2), ('z', 3), ('x', (0,)), ('x', (1,)), ('x', (2,)), ('x', (3,)), ('c', 0), ('c', 1), ('h', 0), ('h', 1), ('a', 0)], 'gates': {}, 'apart': False}


def pick_kernel(n_out, capacity, pods, tokens_hbm, routes_hbm, fixed_hbm, *refs):
    panels, (high, low) = refs[:n_out], refs[n_out : n_out + 2]
    tokens, routes, fixed, sems = refs[n_out + 2 :]
    copies = [
        pltpu.make_async_copy(src, dst, sems.at[i])
        for i, (src, dst) in enumerate(((routes_hbm, routes), (fixed_hbm, fixed), (tokens_hbm, tokens)))
    ]
    for copy in copies:
        copy.start()
    tok_rows = tokens.shape[0]
    rows = lax.broadcasted_iota(jnp.int32, (tok_rows, tok_rows), 0)
    cols = lax.broadcasted_iota(jnp.int32, (tok_rows, tok_rows), 1)
    upto = jnp.where(rows <= cols, 1.0, 0.0).astype(jnp.bfloat16)
    slot_of = lax.broadcasted_iota(jnp.int32, (capacity, tok_rows), 0)
    copies[0].wait()
    hits = [routes[...] == pods[s] for s in range(n_out)]
    live = [jnp.sum(jnp.where(hit, 1.0, 0.0), axis=0, keepdims=True) for hit in hits]
    spare = [jnp.zeros((8 - n_out, tok_rows), jnp.float32)]
    count = jnp.dot(jnp.concatenate(live + spare, axis=0).astype(jnp.bfloat16), upto, preferred_element_type=jnp.float32)
    here = []
    for s in range(n_out):
        slot = jnp.where(live[s] > 0.0, count[s : s + 1].astype(jnp.int32) - 1, -1)
        here.append(slot_of == slot)
    chosen = jnp.concatenate([jnp.where(h, 1.0, 0.0) for h in here], axis=0).astype(jnp.bfloat16)
    copies[2].wait()
    picked = jnp.dot(chosen, tokens[...], preferred_element_type=jnp.float32)
    for s in range(n_out):
        panels[s][...] = picked[s * capacity : (s + 1) * capacity].astype(jnp.bfloat16)
    copies[1].wait()
    for s in range(n_out):
        share = jnp.sum(jnp.where(hits[s], fixed[...], 0), axis=0, keepdims=True)
        spread = jnp.where(here[s], share, 0)
        high[s] = (spread >> 8).astype(jnp.float32)
        low[s] = (spread & 255).astype(jnp.float32)


def pick_call(tokens, routes, fixed, pods, n_out, capacity):
    tok_rows, width = tokens.shape
    vmem = pl.BlockSpec(memory_space=pltpu.VMEM)
    away = pl.BlockSpec(memory_space=pl.ANY)
    outs = [jax.ShapeDtypeStruct((capacity, width), jnp.bfloat16)] * n_out
    outs += [jax.ShapeDtypeStruct((n_out, capacity, tok_rows), jnp.float32)] * 2
    return pl.pallas_call(
        functools.partial(pick_kernel, n_out, capacity),
        in_specs=[pl.BlockSpec(memory_space=pltpu.SMEM), away, away, away],
        out_specs=[vmem] * len(outs),
        out_shape=outs,
        scratch_shapes=[
            pltpu.VMEM(tokens.shape, tokens.dtype),
            pltpu.VMEM(routes.shape[::-1], routes.dtype),
            pltpu.VMEM(fixed.shape[::-1], fixed.dtype),
            pltpu.SemaphoreType.DMA((3,)),
        ],
        compiler_params=pltpu.CompilerParams(vmem_limit_bytes=56 * 1024 * 1024),
        name="pick_rows",
    )(pods, tokens, routes.T, fixed.T)


def combine_kernel(n_out, n_chip, groups, cols, weights, *refs):
    n_in = n_out * n_chip
    landed, traded, out = refs[:n_in], refs[n_in : n_in + len(groups)], refs[n_in + len(groups)]
    own, other, sums, sems, out_sems = refs[n_in + len(groups) + 1 :]
    tok_rows, part_out = sums.shape[1:]
    own_copies = [pltpu.make_async_copy(landed[i].at[0], own.at[i], sems.at[i]) for i in range(n_in)]
    other_copies, first = [], 0
    for i, ref in enumerate(traded):
        count = ref.shape[0]
        other_copies.append(pltpu.make_async_copy(ref, other.at[pl.ds(first, count)], sems.at[n_in + i]))
        first += count
    for copy in own_copies + other_copies:
        copy.start()
    order = [s for steps in groups for s in steps]
    finals = []
    for core in range(2):
        for copy in (own_copies, other_copies)[core]:
            copy.wait()
        for x in range(n_chip):
            if core:
                parts = [other[order.index(s) * n_chip + x] for s in range(n_out)]
            else:
                parts = [own[s * n_chip + x] for s in range(n_out)]
            rows = jnp.concatenate([p.astype(jnp.float32) for p in parts], axis=0).astype(jnp.bfloat16)
            both = jnp.dot(weights[...], rows, preferred_element_type=jnp.float32)
            m = 2 * x + core
            sums[m] = both[:tok_rows] * (1.0 / 256.0) + both[tok_rows:] * (1.0 / 65536.0)
            columns = pl.ds(pl.multiple_of(cols[m] * part_out, 128), part_out)
            finals.append(pltpu.make_async_copy(sums.at[m], out.at[:, columns], out_sems.at[m]))
            finals[-1].start()
    for copy in finals:
        copy.wait()


def combine_call(weights, landed, swaps, cols, n_out, n_chip, capacity, tok_rows):
    arrived = [landed[s, x] for s in range(n_out) for x in range(n_chip)]
    groups = [tuple(steps) for steps, _ in swaps]
    traded = [v for _, v in swaps]
    part_out = traded[0].shape[-1]
    n_loc = 2 * n_chip
    away = pl.BlockSpec(memory_space=pl.ANY)
    return pl.pallas_call(
        functools.partial(combine_kernel, n_out, n_chip, groups),
        in_specs=[pl.BlockSpec(memory_space=pltpu.SMEM), pl.BlockSpec(memory_space=pltpu.VMEM)]
        + [away] * (len(arrived) + len(traded)),
        out_specs=away,
        out_shape=jax.ShapeDtypeStruct((tok_rows, n_loc * part_out), jnp.float32),
        scratch_shapes=[
            pltpu.VMEM((n_out * n_chip, capacity, part_out), jnp.bfloat16),
            pltpu.VMEM((n_out * n_chip, capacity, part_out), jnp.bfloat16),
            pltpu.VMEM((n_loc, tok_rows, part_out), jnp.float32),
            pltpu.SemaphoreType.DMA((len(arrived) + len(traded),)),
            pltpu.SemaphoreType.DMA((n_loc,)),
        ],
        compiler_params=pltpu.CompilerParams(vmem_limit_bytes=16 * 1024 * 1024),
        name="weigh_rows",
    )(cols, weights, *arrived, *traded)


def per_device(tokens, routes, combine_fixed, gate_weight, up_weight, down_weight):
    tok_rows, width = tokens.shape
    n_out = lax.axis_size("outer")
    n_loc = lax.axis_size("local")
    n_chip = n_loc // 2
    capacity = 3 * tok_rows // (2 * n_out)
    part_out = down_weight.shape[2]
    part_hid = gate_weight.shape[2]
    z = lax.axis_index("outer")
    l = lax.axis_index("local")
    gate_local = gate_weight[0]
    up_local = up_weight[0]
    seen = {}
    gates = CFG["gates"]

    def gated(name, value):
        names = [g for g in gates.get(name, ()) if g in seen]
        if names:
            value = lax.optimization_barrier((value,) + tuple(seen[g] for g in names))[0]
        seen[name] = value
        return value

    def down_rows(core):
        return jnp.concatenate(
            [
                lax.dynamic_slice_in_dim(down_weight[0], (l ^ (2 * x + core)) * part_hid, part_hid, 0)
                for x in range(n_chip)
            ],
            axis=0,
        )

    down_same, down_other = down_rows(0), down_rows(1)
    pods = (z ^ jnp.arange(n_out, dtype=jnp.int32)) * EXP_POD

    def places(targets):
        hit_mask = routes[:, :, None] == targets[None, None, :]
        fixed = jnp.sum(jnp.where(hit_mask, combine_fixed[:, :, None], 0), axis=1)
        is_live = jnp.any(hit_mask, axis=1).astype(jnp.int32)
        slot_index = jnp.where(is_live == 1, jnp.cumsum(is_live, axis=0) - 1, -1)
        placing = slot_index[:, :, None] == jnp.arange(capacity, dtype=jnp.int32)[None, None, :]
        return placing, fixed

    def pod_weights(targets):
        placing, fixed = places(targets)
        spread = jnp.where(placing, fixed[:, :, None], 0).reshape(tok_rows, -1)
        return (spread >> 8).astype(jnp.bfloat16), (spread & 255).astype(jnp.bfloat16)

    in_kernels = False and capacity % 8 == 0 and part_out % 128 == 0
    if in_kernels:
        *panels, high, low = pick_call(tokens, routes, combine_fixed, pods, n_out, capacity)
        high = high.reshape(-1, tok_rows).T.astype(jnp.bfloat16)
        low = low.reshape(-1, tok_rows).T.astype(jnp.bfloat16)
    else:
        placing, fixed = places(pods)
        panels = jnp.einsum(
            "tqc,td->qcd", placing.astype(jnp.bfloat16), tokens, preferred_element_type=jnp.float32
        ).astype(jnp.bfloat16)
        panels = panels.reshape(4, -1, width)
        spread = jnp.where(placing, fixed[:, :, None], 0).reshape(tok_rows, -1)
        high = (spread >> 8).astype(jnp.bfloat16)
        low = (spread & 255).astype(jnp.bfloat16)

    span = n_out // 4

    def by_pod(v, s, axis, move):
        if span == 1:
            return move(v, s) if s else v
        parts = jnp.split(v, span, axis=axis)
        parts = [move(p, s * span + i) if s * span + i else p for i, p in enumerate(parts)]
        return jnp.concatenate(parts, axis=axis)

    def outer_xor(v, s, axis):
        return by_pod(v, s, axis, lambda p, t: lax.ppermute(p, "outer", [(i, i ^ t) for i in range(n_out)]))

    def local_xor(v, m):
        return lax.ppermute(v, "local", [(i, i ^ m) for i in range(n_loc)])

    def both_xor(v, s, m):
        if m == 0:
            return outer_xor(v, s, 1)

        def move(p, t):
            pairs = [(a * n_loc + b, (a ^ t) * n_loc + (b ^ m)) for a in range(n_out) for b in range(n_loc)]
            return lax.ppermute(p, ("outer", "local"), pairs)

        if span == 1:
            return move(v, s)
        parts = jnp.split(v, span, axis=1)
        return jnp.concatenate([move(p, s * span + i) for i, p in enumerate(parts)], axis=1)

    def first_half(rows):
        gate_proj = jnp.dot(rows, gate_local, preferred_element_type=jnp.float32)
        up_proj = jnp.dot(rows, up_local, preferred_element_type=jnp.float32)
        return (jax.nn.silu(gate_proj) * up_proj).astype(jnp.bfloat16)

    chip_of = {}
    hid = []
    outs = {}
    landed = {}
    pieces = {}
    back = {}
    shared = []
    swaps = []
    mine = {}
    todo = list(CFG["order"])
    for item in todo:
        kind, arg = item
        if kind == "z":
            s = arg
            mine[s] = gated(f"zd{s}", outer_xor(gated(f"zs{s}", panels[s]), s, 0))
        elif kind == "x":
            for s in arg:
                chip_of[s, 0] = mine[s]
            for x in range(1, n_chip):
                held = [mine[s] for s in arg]
                held = held[0] if len(arg) == 1 else jnp.stack(held)
                got = gated(f"xd{arg[0]}{x}", local_xor(gated(f"xs{arg[0]}{x}", held), 2 * x))
                for at, s in enumerate(arg):
                    chip_of[s, x] = got if len(arg) == 1 else got[at]
        elif kind == "c":
            steps = CFG["C"][arg]
            if CFG["apart"]:
                sides = []
                for x in range(n_chip):
                    same = jnp.concatenate([chip_of[s, x] for s in steps], axis=0)
                    other = gated(f"cd{arg}{x}", local_xor(gated(f"cs{arg}{x}", same), 1))
                    sides.append(first_half(jnp.concatenate([same, other], axis=0)).reshape(2, -1, part_hid))
                hid.append((arg, jnp.stack(sides)))
            else:
                same = jnp.concatenate([chip_of[s, x] for x in range(n_chip) for s in steps], axis=0)
                other = gated(f"cd{arg}", local_xor(gated(f"cs{arg}", same), 1))
                halves = [first_half(rows).reshape(n_chip, -1, part_hid) for rows in (same, other)]
                hid.append((arg, jnp.stack(halves, axis=1)))
        elif kind == "h":
            cs = CFG["H"][arg]
            steps = [s for c in cs for s in CFG["C"][c]]
            count = len(steps)
            hd = dict(hid)
            hidden = jnp.concatenate([hd[c] for c in cs], axis=2)
            hidden = gated(f"hs{arg}", hidden)
            sides = []
            for x in range(n_chip):
                side = hidden if x == 0 else gated(f"hd{arg}{x}", local_xor(hidden, 2 * x))
                sides.append(jnp.concatenate([side[y ^ x : (y ^ x) + 1] for y in range(n_chip)], axis=0))
            hidden_same = jnp.concatenate(sides, axis=3).reshape(2 * n_chip * count * span * capacity, n_chip * part_hid)
            hidden_other = gated(f"kd{arg}", local_xor(gated(f"ks{arg}", hidden_same), 1))
            out_same = jnp.dot(hidden_same, down_same, preferred_element_type=jnp.float32)
            out_other = jnp.dot(hidden_other, down_other, preferred_element_type=jnp.float32)
            out_other = out_other.reshape(n_chip, 2, -1, part_out)
            out_other = jnp.concatenate([out_other[:, 1:], out_other[:, :1]], axis=1).reshape(out_same.shape)
            expert_out = (out_same + out_other).astype(jnp.bfloat16)
            expert_out = expert_out.reshape(n_chip, 2, count, span * capacity, part_out)
            for at, s in enumerate(steps):
                outs[s] = expert_out[:, :, at]
        elif kind == "r":
            s = arg
            for x in range(n_chip):
                landed[s, x] = gated(f"rd{s}{x}", both_xor(gated(f"rs{s}{x}", outs[s][x]), s, 2 * x))
        elif kind == "t":
            for x in range(n_chip):
                block = jnp.stack([outs[s][x] for s in arg], axis=1)
                if x:
                    block = gated(f"td{arg[0]}{x}", local_xor(gated(f"ts{arg[0]}{x}", block), 2 * x))
                for at, s in enumerate(arg):
                    landed[s, x] = block[:, at]
            for s in arg:
                if s or span > 1:
                    moved = outer_xor(gated(f"rs{s}0", jnp.stack([landed[s, x] for x in range(n_chip)])), s, 2)
                    moved = gated(f"rd{s}0", moved)
                    for x in range(n_chip):
                        landed[s, x] = moved[x]
        elif kind == "a":
            parts = []
            for s in range(4):
                block = outs[s].reshape(n_loc, span, capacity, part_out)
                parts.append(block.transpose(1, 0, 2, 3) if span > 1 else block.reshape(1, *block.shape[:1], *block.shape[2:]))
            blocks = jnp.concatenate(parts, axis=0).reshape(n_out * n_loc, capacity, part_out)
            place = z * n_loc + l
            blocks = jnp.concatenate(
                [lax.dynamic_slice_in_dim(blocks, place ^ i, 1, 0) for i in range(n_out * n_loc)], axis=0
            )
            blocks = lax.all_to_all(blocks, ("outer", "local"), split_axis=0, concat_axis=0, tiled=True)
            blocks = blocks.reshape(n_out, n_loc, capacity, part_out)
            weights = jnp.concatenate(pod_weights(jnp.arange(n_out, dtype=jnp.int32) * EXP_POD), axis=0)
            returned = blocks.transpose(0, 2, 1, 3).reshape(n_out * capacity, width)
            both = jnp.dot(weights, returned, preferred_element_type=jnp.float32)
            return both[:tok_rows] * (1.0 / 256.0) + both[tok_rows:] * (1.0 / 65536.0)
        elif kind == "q":
            a, b = arg
            core = l & 1
            kept = jnp.where(core == 0, outs[a], outs[b])
            given = gated(f"qs{a}", jnp.where(core == 0, outs[b], outs[a])[:, ::-1])
            taken = gated(f"qd{a}", local_xor(given, 1))
            for x in range(n_chip):
                block = gated(f"us{a}{x}", jnp.stack([kept[x], taken[x]]))

                def move(p, i, x=x):
                    pairs = []
                    for zz in range(n_out):
                        for ll in range(n_loc):
                            t = (b if ll & 1 else a) * span + i
                            pairs.append((zz * n_loc + ll, (zz ^ t) * n_loc + (ll ^ (2 * x))))
                    return lax.ppermute(p, ("outer", "local"), pairs)

                parts = [move(p, i) for i, p in enumerate(jnp.split(block, span, axis=2) if span > 1 else [block])]
                back[a, x] = gated(f"ud{a}{x}", parts[0] if span == 1 else jnp.concatenate(parts, axis=2))
        elif kind == "v":
            stack = jnp.stack([back[a, x][:, 1] for a, b in arg for x in range(n_chip)])
            swapped = gated(f"wd{arg[0][0]}", local_xor(gated(f"ws{arg[0][0]}", stack), 1))
            for at, (a, b) in enumerate(arg):
                for x in range(n_chip):
                    pieces[a, 2 * x] = back[a, x][0, 0]
                    pieces[a, 2 * x + 1] = back[a, x][1, 0]
                    pieces[b, 2 * x] = swapped[at * n_chip + x, 1]
                    pieces[b, 2 * x + 1] = swapped[at * n_chip + x, 0]
                shared.append((a, b))
        elif kind == "w":
            steps = arg
            stack = gated(f"ws{steps[0]}", jnp.stack([landed[s, x][1] for s in steps for x in range(n_chip)]))
            swapped = gated(f"wd{steps[0]}", local_xor(stack, 1))
            for at, s in enumerate(steps):
                for x in range(n_chip):
                    pieces[s, 2 * x] = landed[s, x][0]
                    pieces[s, 2 * x + 1] = swapped[at * n_chip + x]
            swaps.append((steps, swapped))

    if in_kernels:
        cols = l ^ jnp.arange(n_loc, dtype=jnp.int32)
        weights = jnp.concatenate([high, low], axis=0)
        return combine_call(weights, landed, swaps, cols, n_out, n_chip, capacity, tok_rows)
    def in_turn(w):
        cuts = jnp.split(w, 4, axis=1)
        for a, b in shared:
            cuts[a], cuts[b] = (jnp.where((l & 1) == 0, cuts[i], cuts[j]) for i, j in ((a, b), (b, a)))
        return jnp.concatenate(cuts, axis=1)

    high, low = in_turn(high), in_turn(low)
    combined = jnp.zeros((tok_rows, width), jnp.float32)
    for m in range(n_loc):
        returned = jnp.concatenate([pieces[s, m] for s in range(4)], axis=0)
        block = jnp.dot(high, returned, preferred_element_type=jnp.float32) * (1.0 / 256.0)
        block += jnp.dot(low, returned, preferred_element_type=jnp.float32) * (1.0 / 65536.0)
        combined = lax.dynamic_update_slice(combined, block, (0, (l ^ m) * part_out))
    return combined


def solution(mesh):
    in_specs = (
        P(("groups", "outer", "local"), None),
        P(("groups", "outer", "local"), None),
        P(("groups", "outer", "local"), None),
        P("outer", None, "local"),
        P("outer", None, "local"),
        P("outer", None, "local"),
    )
    out_specs = P(("groups", "outer", "local"), None)
    return jax.shard_map(
        per_device, mesh=mesh, in_specs=in_specs, out_specs=out_specs, check_vma=False
    )
```

```python
import jax
import jax.numpy as jnp
from jax import lax
from jax.experimental import pallas as pl
from jax.experimental.pallas import tpu as pltpu
from jax.sharding import PartitionSpec as P
import functools

EXP_POD = 8
CFG = {'C': [[0, 1], [2, 3]], 'H': [[0], [1]], 'order': [('z', 0), ('z', 1), ('z', 2), ('z', 3), ('x', (0,)), ('x', (1,)), ('c', 0), ('x', (2,)), ('x', (3,)), ('h', 0), ('c', 1), ('h', 1), ('r', 2), ('r', 3), ('t', (0, 1)), ('w', (0, 1, 2, 3))], 'gates': {'rd10': ['rd20', 'rd21', 'rd30', 'rd31'], 'rs10': ['hd11'], 'xs21': ['cd0'], 'xs31': ['cd0'], 'ks0': ['xd21', 'xd31'], 'ts01': ['cd1']}, 'apart': False}


def pick_kernel(n_out, capacity, pods, tokens_hbm, routes_hbm, fixed_hbm, *refs):
    panels, (high, low) = refs[:n_out], refs[n_out : n_out + 2]
    tokens, routes, fixed, sems = refs[n_out + 2 :]
    copies = [
        pltpu.make_async_copy(src, dst, sems.at[i])
        for i, (src, dst) in enumerate(((routes_hbm, routes), (fixed_hbm, fixed), (tokens_hbm, tokens)))
    ]
    for copy in copies:
        copy.start()
    tok_rows = tokens.shape[0]
    rows = lax.broadcasted_iota(jnp.int32, (tok_rows, tok_rows), 0)
    cols = lax.broadcasted_iota(jnp.int32, (tok_rows, tok_rows), 1)
    upto = jnp.where(rows <= cols, 1.0, 0.0).astype(jnp.bfloat16)
    slot_of = lax.broadcasted_iota(jnp.int32, (capacity, tok_rows), 0)
    copies[0].wait()
    hits = [routes[...] == pods[s] for s in range(n_out)]
    live = [jnp.sum(jnp.where(hit, 1.0, 0.0), axis=0, keepdims=True) for hit in hits]
    spare = [jnp.zeros((8 - n_out, tok_rows), jnp.float32)]
    count = jnp.dot(jnp.concatenate(live + spare, axis=0).astype(jnp.bfloat16), upto, preferred_element_type=jnp.float32)
    here = []
    for s in range(n_out):
        slot = jnp.where(live[s] > 0.0, count[s : s + 1].astype(jnp.int32) - 1, -1)
        here.append(slot_of == slot)
    chosen = jnp.concatenate([jnp.where(h, 1.0, 0.0) for h in here], axis=0).astype(jnp.bfloat16)
    copies[2].wait()
    picked = jnp.dot(chosen, tokens[...], preferred_element_type=jnp.float32)
    for s in range(n_out):
        panels[s][...] = picked[s * capacity : (s + 1) * capacity].astype(jnp.bfloat16)
    copies[1].wait()
    for s in range(n_out):
        share = jnp.sum(jnp.where(hits[s], fixed[...], 0), axis=0, keepdims=True)
        spread = jnp.where(here[s], share, 0)
        high[s] = (spread >> 8).astype(jnp.float32)
        low[s] = (spread & 255).astype(jnp.float32)


def pick_call(tokens, routes, fixed, pods, n_out, capacity):
    tok_rows, width = tokens.shape
    vmem = pl.BlockSpec(memory_space=pltpu.VMEM)
    away = pl.BlockSpec(memory_space=pl.ANY)
    outs = [jax.ShapeDtypeStruct((capacity, width), jnp.bfloat16)] * n_out
    outs += [jax.ShapeDtypeStruct((n_out, capacity, tok_rows), jnp.float32)] * 2
    return pl.pallas_call(
        functools.partial(pick_kernel, n_out, capacity),
        in_specs=[pl.BlockSpec(memory_space=pltpu.SMEM), away, away, away],
        out_specs=[vmem] * len(outs),
        out_shape=outs,
        scratch_shapes=[
            pltpu.VMEM(tokens.shape, tokens.dtype),
            pltpu.VMEM(routes.shape[::-1], routes.dtype),
            pltpu.VMEM(fixed.shape[::-1], fixed.dtype),
            pltpu.SemaphoreType.DMA((3,)),
        ],
        compiler_params=pltpu.CompilerParams(vmem_limit_bytes=56 * 1024 * 1024),
        name="pick_rows",
    )(pods, tokens, routes.T, fixed.T)


def combine_kernel(n_out, n_chip, groups, cols, weights, *refs):
    n_in = n_out * n_chip
    landed, traded, out = refs[:n_in], refs[n_in : n_in + len(groups)], refs[n_in + len(groups)]
    own, other, sums, sems, out_sems = refs[n_in + len(groups) + 1 :]
    tok_rows, part_out = sums.shape[1:]
    own_copies = [pltpu.make_async_copy(landed[i].at[0], own.at[i], sems.at[i]) for i in range(n_in)]
    other_copies, first = [], 0
    for i, ref in enumerate(traded):
        count = ref.shape[0]
        other_copies.append(pltpu.make_async_copy(ref, other.at[pl.ds(first, count)], sems.at[n_in + i]))
        first += count
    for copy in own_copies + other_copies:
        copy.start()
    order = [s for steps in groups for s in steps]
    finals = []
    for core in range(2):
        for copy in (own_copies, other_copies)[core]:
            copy.wait()
        for x in range(n_chip):
            if core:
                parts = [other[order.index(s) * n_chip + x] for s in range(n_out)]
            else:
                parts = [own[s * n_chip + x] for s in range(n_out)]
            rows = jnp.concatenate([p.astype(jnp.float32) for p in parts], axis=0).astype(jnp.bfloat16)
            both = jnp.dot(weights[...], rows, preferred_element_type=jnp.float32)
            m = 2 * x + core
            sums[m] = both[:tok_rows] * (1.0 / 256.0) + both[tok_rows:] * (1.0 / 65536.0)
            columns = pl.ds(pl.multiple_of(cols[m] * part_out, 128), part_out)
            finals.append(pltpu.make_async_copy(sums.at[m], out.at[:, columns], out_sems.at[m]))
            finals[-1].start()
    for copy in finals:
        copy.wait()


def combine_call(weights, landed, swaps, cols, n_out, n_chip, capacity, tok_rows):
    arrived = [landed[s, x] for s in range(n_out) for x in range(n_chip)]
    groups = [tuple(steps) for steps, _ in swaps]
    traded = [v for _, v in swaps]
    part_out = traded[0].shape[-1]
    n_loc = 2 * n_chip
    away = pl.BlockSpec(memory_space=pl.ANY)
    return pl.pallas_call(
        functools.partial(combine_kernel, n_out, n_chip, groups),
        in_specs=[pl.BlockSpec(memory_space=pltpu.SMEM), pl.BlockSpec(memory_space=pltpu.VMEM)]
        + [away] * (len(arrived) + len(traded)),
        out_specs=away,
        out_shape=jax.ShapeDtypeStruct((tok_rows, n_loc * part_out), jnp.float32),
        scratch_shapes=[
            pltpu.VMEM((n_out * n_chip, capacity, part_out), jnp.bfloat16),
            pltpu.VMEM((n_out * n_chip, capacity, part_out), jnp.bfloat16),
            pltpu.VMEM((n_loc, tok_rows, part_out), jnp.float32),
            pltpu.SemaphoreType.DMA((len(arrived) + len(traded),)),
            pltpu.SemaphoreType.DMA((n_loc,)),
        ],
        compiler_params=pltpu.CompilerParams(vmem_limit_bytes=16 * 1024 * 1024),
        name="weigh_rows",
    )(cols, weights, *arrived, *traded)


def per_device(tokens, routes, combine_fixed, gate_weight, up_weight, down_weight):
    tok_rows, width = tokens.shape
    n_out = lax.axis_size("outer")
    n_loc = lax.axis_size("local")
    n_chip = n_loc // 2
    capacity = 3 * tok_rows // (2 * n_out)
    part_out = down_weight.shape[2]
    part_hid = gate_weight.shape[2]
    z = lax.axis_index("outer")
    l = lax.axis_index("local")
    gate_local = gate_weight[0]
    up_local = up_weight[0]
    seen = {}
    gates = CFG["gates"]

    def gated(name, value):
        names = [g for g in gates.get(name, ()) if g in seen]
        if names:
            value = lax.optimization_barrier((value,) + tuple(seen[g] for g in names))[0]
        seen[name] = value
        return value

    def down_rows(core):
        return jnp.concatenate(
            [
                lax.dynamic_slice_in_dim(down_weight[0], (l ^ (2 * x + core)) * part_hid, part_hid, 0)
                for x in range(n_chip)
            ],
            axis=0,
        )

    down_same, down_other = down_rows(0), down_rows(1)
    pods = (z ^ jnp.arange(n_out, dtype=jnp.int32)) * EXP_POD
    in_kernels = False and capacity % 8 == 0 and part_out % 128 == 0
    if in_kernels:
        *panels, high, low = pick_call(tokens, routes, combine_fixed, pods, n_out, capacity)
        high = high.reshape(-1, tok_rows).T.astype(jnp.bfloat16)
        low = low.reshape(-1, tok_rows).T.astype(jnp.bfloat16)
    else:
        hit_mask = routes[:, :, None] == pods[None, None, :]
        fixed = jnp.sum(jnp.where(hit_mask, combine_fixed[:, :, None], 0), axis=1)
        is_live = jnp.any(hit_mask, axis=1).astype(jnp.int32)
        slot_index = jnp.where(is_live == 1, jnp.cumsum(is_live, axis=0) - 1, -1)
        placing = slot_index[:, :, None] == jnp.arange(capacity, dtype=jnp.int32)[None, None, :]
        panels = jnp.einsum(
            "tqc,td->qcd", placing.astype(jnp.bfloat16), tokens, preferred_element_type=jnp.float32
        ).astype(jnp.bfloat16)
        panels = panels.reshape(4, -1, width)
        spread = jnp.where(placing, fixed[:, :, None], 0).reshape(tok_rows, -1)
        high = (spread >> 8).astype(jnp.bfloat16)
        low = (spread & 255).astype(jnp.bfloat16)

    span = n_out // 4

    def by_pod(v, s, axis, move):
        if span == 1:
            return move(v, s) if s else v
        parts = jnp.split(v, span, axis=axis)
        parts = [move(p, s * span + i) if s * span + i else p for i, p in enumerate(parts)]
        return jnp.concatenate(parts, axis=axis)

    def outer_xor(v, s, axis):
        return by_pod(v, s, axis, lambda p, t: lax.ppermute(p, "outer", [(i, i ^ t) for i in range(n_out)]))

    def local_xor(v, m):
        return lax.ppermute(v, "local", [(i, i ^ m) for i in range(n_loc)])

    def both_xor(v, s, m):
        if m == 0:
            return outer_xor(v, s, 1)

        def move(p, t):
            pairs = [(a * n_loc + b, (a ^ t) * n_loc + (b ^ m)) for a in range(n_out) for b in range(n_loc)]
            return lax.ppermute(p, ("outer", "local"), pairs)

        if span == 1:
            return move(v, s)
        parts = jnp.split(v, span, axis=1)
        return jnp.concatenate([move(p, s * span + i) for i, p in enumerate(parts)], axis=1)

    def first_half(rows):
        gate_proj = jnp.dot(rows, gate_local, preferred_element_type=jnp.float32)
        up_proj = jnp.dot(rows, up_local, preferred_element_type=jnp.float32)
        return (jax.nn.silu(gate_proj) * up_proj).astype(jnp.bfloat16)

    chip_of = {}
    hid = []
    outs = {}
    landed = {}
    pieces = {}
    back = {}
    shared = []
    swaps = []
    mine = {}
    todo = list(CFG["order"])
    for item in todo:
        kind, arg = item
        if kind == "z":
            s = arg
            mine[s] = gated(f"zd{s}", outer_xor(gated(f"zs{s}", panels[s]), s, 0))
        elif kind == "x":
            for s in arg:
                chip_of[s, 0] = mine[s]
            for x in range(1, n_chip):
                held = [mine[s] for s in arg]
                held = held[0] if len(arg) == 1 else jnp.stack(held)
                got = gated(f"xd{arg[0]}{x}", local_xor(gated(f"xs{arg[0]}{x}", held), 2 * x))
                for at, s in enumerate(arg):
                    chip_of[s, x] = got if len(arg) == 1 else got[at]
        elif kind == "c":
            steps = CFG["C"][arg]
            if CFG["apart"]:
                sides = []
                for x in range(n_chip):
                    same = jnp.concatenate([chip_of[s, x] for s in steps], axis=0)
                    other = gated(f"cd{arg}{x}", local_xor(gated(f"cs{arg}{x}", same), 1))
                    sides.append(first_half(jnp.concatenate([same, other], axis=0)).reshape(2, -1, part_hid))
                hid.append((arg, jnp.stack(sides)))
            else:
                same = jnp.concatenate([chip_of[s, x] for x in range(n_chip) for s in steps], axis=0)
                other = gated(f"cd{arg}", local_xor(gated(f"cs{arg}", same), 1))
                halves = [first_half(rows).reshape(n_chip, -1, part_hid) for rows in (same, other)]
                hid.append((arg, jnp.stack(halves, axis=1)))
        elif kind == "h":
            cs = CFG["H"][arg]
            steps = [s for c in cs for s in CFG["C"][c]]
            count = len(steps)
            hd = dict(hid)
            hidden = jnp.concatenate([hd[c] for c in cs], axis=2)
            hidden = gated(f"hs{arg}", hidden)
            sides = []
            for x in range(n_chip):
                side = hidden if x == 0 else gated(f"hd{arg}{x}", local_xor(hidden, 2 * x))
                sides.append(jnp.concatenate([side[y ^ x : (y ^ x) + 1] for y in range(n_chip)], axis=0))
            hidden_same = jnp.concatenate(sides, axis=3).reshape(2 * n_chip * count * span * capacity, n_chip * part_hid)
            hidden_other = gated(f"kd{arg}", local_xor(gated(f"ks{arg}", hidden_same), 1))
            out_same = jnp.dot(hidden_same, down_same, preferred_element_type=jnp.float32)
            out_other = jnp.dot(hidden_other, down_other, preferred_element_type=jnp.float32)
            out_other = out_other.reshape(n_chip, 2, -1, part_out)
            out_other = jnp.concatenate([out_other[:, 1:], out_other[:, :1]], axis=1).reshape(out_same.shape)
            expert_out = (out_same + out_other).astype(jnp.bfloat16)
            expert_out = expert_out.reshape(n_chip, 2, count, span * capacity, part_out)
            for at, s in enumerate(steps):
                outs[s] = expert_out[:, :, at]
        elif kind == "r":
            s = arg
            for x in range(n_chip):
                landed[s, x] = gated(f"rd{s}{x}", both_xor(gated(f"rs{s}{x}", outs[s][x]), s, 2 * x))
        elif kind == "t":
            for x in range(n_chip):
                block = jnp.stack([outs[s][x] for s in arg], axis=1)
                if x:
                    block = gated(f"td{arg[0]}{x}", local_xor(gated(f"ts{arg[0]}{x}", block), 2 * x))
                for at, s in enumerate(arg):
                    landed[s, x] = block[:, at]
            for s in arg:
                if s or span > 1:
                    moved = outer_xor(gated(f"rs{s}0", jnp.stack([landed[s, x] for x in range(n_chip)])), s, 2)
                    moved = gated(f"rd{s}0", moved)
                    for x in range(n_chip):
                        landed[s, x] = moved[x]
        elif kind == "q":
            a, b = arg
            core = l & 1
            kept = jnp.where(core == 0, outs[a], outs[b])
            given = gated(f"qs{a}", jnp.where(core == 0, outs[b], outs[a])[:, ::-1])
            taken = gated(f"qd{a}", local_xor(given, 1))
            for x in range(n_chip):
                block = gated(f"us{a}{x}", jnp.stack([kept[x], taken[x]]))

                def move(p, i, x=x):
                    pairs = []
                    for zz in range(n_out):
                        for ll in range(n_loc):
                            t = (b if ll & 1 else a) * span + i
                            pairs.append((zz * n_loc + ll, (zz ^ t) * n_loc + (ll ^ (2 * x))))
                    return lax.ppermute(p, ("outer", "local"), pairs)

                parts = [move(p, i) for i, p in enumerate(jnp.split(block, span, axis=2) if span > 1 else [block])]
                back[a, x] = gated(f"ud{a}{x}", parts[0] if span == 1 else jnp.concatenate(parts, axis=2))
        elif kind == "v":
            stack = jnp.stack([back[a, x][:, 1] for a, b in arg for x in range(n_chip)])
            swapped = gated(f"wd{arg[0][0]}", local_xor(gated(f"ws{arg[0][0]}", stack), 1))
            for at, (a, b) in enumerate(arg):
                for x in range(n_chip):
                    pieces[a, 2 * x] = back[a, x][0, 0]
                    pieces[a, 2 * x + 1] = back[a, x][1, 0]
                    pieces[b, 2 * x] = swapped[at * n_chip + x, 1]
                    pieces[b, 2 * x + 1] = swapped[at * n_chip + x, 0]
                shared.append((a, b))
        elif kind == "w":
            steps = arg
            stack = gated(f"ws{steps[0]}", jnp.stack([landed[s, x][1] for s in steps for x in range(n_chip)]))
            swapped = gated(f"wd{steps[0]}", local_xor(stack, 1))
            for at, s in enumerate(steps):
                for x in range(n_chip):
                    pieces[s, 2 * x] = landed[s, x][0]
                    pieces[s, 2 * x + 1] = swapped[at * n_chip + x]
            swaps.append((steps, swapped))

    if in_kernels:
        cols = l ^ jnp.arange(n_loc, dtype=jnp.int32)
        weights = jnp.concatenate([high, low], axis=0)
        return combine_call(weights, landed, swaps, cols, n_out, n_chip, capacity, tok_rows)
    def in_turn(w):
        cuts = jnp.split(w, 4, axis=1)
        for a, b in shared:
            cuts[a], cuts[b] = (jnp.where((l & 1) == 0, cuts[i], cuts[j]) for i, j in ((a, b), (b, a)))
        return jnp.concatenate(cuts, axis=1)

    high, low = in_turn(high), in_turn(low)
    combined = jnp.zeros((tok_rows, width), jnp.float32)
    for m in range(n_loc):
        returned = jnp.concatenate([pieces[s, m] for s in range(4)], axis=0)
        block = jnp.dot(high, returned, preferred_element_type=jnp.float32) * (1.0 / 256.0)
        block += jnp.dot(low, returned, preferred_element_type=jnp.float32) * (1.0 / 65536.0)
        combined = lax.dynamic_update_slice(combined, block, (0, (l ^ m) * part_out))
    return combined


def solution(mesh):
    in_specs = (
        P(("groups", "outer", "local"), None),
        P(("groups", "outer", "local"), None),
        P(("groups", "outer", "local"), None),
        P("outer", None, "local"),
        P("outer", None, "local"),
        P("outer", None, "local"),
    )
    out_specs = P(("groups", "outer", "local"), None)
    return jax.shard_map(
        per_device, mesh=mesh, in_specs=in_specs, out_specs=out_specs, check_vma=False
    )
```
